512 devices in a mesh: row: 4 (over x), col: 16 (over y, z_hi, core), ch: 8 (over z_lo).
Axes of the slice: x: 4, y: 4, z: 16 (z_hi: 2, z_lo: 8; z = z_hi * 8 + z_lo), core: 2. Of those that a mesh axis runs over, the one named last changes fastest.
Arguments:
- pair: bfloat16 [512, 512, 128], P('col', 'row'), may hold values from -6 to 6
- token_mask: int32 [512], replicated, may hold values 0 or 1
- pair_mask: int32 [512, 512], P('col', 'row'), may hold values 0 or 1
- ln_gain: float32 [128], replicated, may hold values from 0.5 to 1.5
- w_in: bfloat16 [128, 4, 128], P(None, None, 'ch'), may hold values from -0.5 to 0.5
- grad_tri: bfloat16 [128, 512, 512], P('ch', 'col'), may hold values from -0.29882812 to 0.29882812
Outputs:
- d_pair: bfloat16 [512, 512, 128], P('col', 'row')
- w_grad: float32 [128, 4, 128], P(None, None, 'ch')
The draws below stay inside these ranges and needn't reach their ends.
All inputs are finite; a program needn't handle non-finite values. No bound on the sum of `pair_mask` on one device may be relied on, other than what follows from the above.
Results may differ from the reference program's by a relative error of at most 0.012.
Values may be sent and summed in bfloat16 or wider, within the bound.
A program may use at most 64 MiB of HBM per device.

```python
import jax
import jax.numpy as jnp
from jax import lax

C = 128
H = 128
N = 512


def place_ends(array, stream_key, least, top_value):
    longest = array.shape.index(max(array.shape))
    spots = []
    for shift in (0, 1):
        where = [jax.random.randint(jax.random.fold_in(stream_key, axis), (), 0, length) for axis, length in enumerate(array.shape)]
        where[longest] = (where[longest] + shift) % array.shape[longest]
        spots.append(tuple(where))
    return array.at[spots[0]].set(least).at[spots[1]].set(top_value)


def levels(rng, dims, split, smallest, top_value):
    def one(axis_at, blocks):
        draws = jax.random.uniform(jax.random.fold_in(jax.random.fold_in(rng, 6), axis_at), (blocks,), jnp.float32, smallest / len(split), top_value / len(split))
        return jnp.repeat(jnp.exp(draws), dims[axis_at] // blocks).reshape((-1,) + (1,) * (len(dims) - axis_at - 1))

    gain = one(*split[0])
    for cut in split[1:]:
        gain = gain * one(*cut)
    return gain


def bell_draw(own_key, shape, scale, bound, cuts=(), dtype=jnp.bfloat16):
    level = levels(own_key, shape, cuts, -0.22, 0.18) if cuts else 1.0
    entries = jax.random.normal(own_key, shape, jnp.float32) * scale * level
    return jnp.minimum(jnp.maximum(entries, -bound), bound).astype(dtype)


def setup_inputs(seed: int = 0) -> dict:
    seeds = jax.random.split(jax.random.key(seed), 7)
    pair = bell_draw(seeds[0], (N, N, C), 1.0, 6.0, ((0, 16), (1, 4)))
    token_mask = place_ends((jax.random.randint(seeds[1], (N,), 0, 8) < 7).astype(jnp.int32), jax.random.fold_in(seeds[1], 1), 0, 1)
    pair_mask = place_ends((jax.random.randint(seeds[2], (N, N), 0, 8) < 7).astype(jnp.int32), jax.random.fold_in(seeds[2], 1), 0, 1)
    ln_gain = jnp.clip(1.0 + 0.1 * jax.random.normal(seeds[3], (C,), jnp.float32), 0.5, 1.5)
    w_in = bell_draw(seeds[4], (C, 4, H), C ** -0.5, 0.5, ((2, 8),))
    grad_tri = bell_draw(seeds[5], (H, N, N), 0.05, 0.29882812, ((0, 8), (1, 16)))
    return dict(pair=pair, token_mask=token_mask, pair_mask=pair_mask, ln_gain=ln_gain, w_in=w_in, grad_tri=grad_tri)


EPS = 1e-05

def layer_stats(pair, ln_gain):
    values = pair.astype(jnp.float32)
    mean_val = lax.optimization_barrier(jnp.mean(values, axis=-1, keepdims=True))
    centred = values - mean_val
    inv_std = lax.rsqrt(lax.optimization_barrier(jnp.mean(centred * centred, axis=-1, keepdims=True)) + EPS)
    standard = centred * inv_std
    normed = (standard * ln_gain).astype(jnp.bfloat16)
    return (standard, inv_std, normed)

def gated(proj, masking):
    sig_left = jax.nn.sigmoid(proj[1])
    sig_right = jax.nn.sigmoid(proj[3])
    left = (masking * sig_left * proj[0]).astype(jnp.bfloat16)
    right = (masking * sig_right * proj[2]).astype(jnp.bfloat16)
    return (left, right, sig_left, sig_right)

def input_grads(proj, masking, sig_left, sig_right, d_left, d_right):
    grad_l = d_left.astype(jnp.float32) * masking
    grad_r = d_right.astype(jnp.float32) * masking
    stacked = jnp.stack([grad_l * sig_left, grad_l * proj[0] * sig_left * (1.0 - sig_left), grad_r * sig_right, grad_r * proj[2] * sig_right * (1.0 - sig_right)])
    return stacked.astype(jnp.bfloat16)

def norm_back(d_norm, standard, inv_std, ln_gain):
    scaled = d_norm * ln_gain
    first = lax.optimization_barrier(jnp.mean(scaled, axis=-1, keepdims=True))
    second = lax.optimization_barrier(jnp.mean(scaled * standard, axis=-1, keepdims=True))
    return (inv_std * (scaled - first - standard * second)).astype(jnp.bfloat16)

def reference(pair, token_mask, pair_mask, ln_gain, w_in, grad_tri):
    standard, inv_std, normed = layer_stats(pair, ln_gain)
    weights = w_in.astype(jnp.float32)
    proj = jnp.einsum('ikc,cgh->ghik', normed.astype(jnp.float32), weights)
    tokens_f = token_mask.astype(jnp.float32)
    masking = pair_mask.astype(jnp.float32) * tokens_f[:, None] * tokens_f[None, :]
    left, right, sig_left, sig_right = gated(proj, masking)
    grad_f = grad_tri.astype(jnp.float32)
    d_left = jnp.einsum('hij,hjk->hik', grad_f, right.astype(jnp.float32)).astype(jnp.bfloat16)
    d_right = jnp.einsum('hij,hik->hjk', grad_f, left.astype(jnp.float32)).astype(jnp.bfloat16)
    grads = input_grads(proj, masking, sig_left, sig_right, d_left, d_right)
    grads_f = grads.astype(jnp.float32)
    d_norm = jnp.einsum('ghik,cgh->ikc', grads_f, weights)
    w_grad = jnp.einsum('ikc,ghik->cgh', normed.astype(jnp.float32), grads_f) / N
    d_pair = norm_back(d_norm, standard, inv_std, ln_gain)
    return (d_pair, w_grad)
```

```python
import functools

import jax
import jax.numpy as jnp
from jax import lax
from jax.experimental import pallas as pl
from jax.experimental.pallas import tpu as pltpu
from jax.sharding import PartitionSpec as P

EPS = 1e-05
F32 = jnp.float32
BF16 = jnp.bfloat16
MESH = pl.DeviceIdType.MESH
NT = (((1,), (1,)), ((), ()))
TN = (((0,), (0,)), ((), ()))


def normalise(x):
    mean = jnp.mean(x, axis=-1, keepdims=True)
    cen = x - mean
    inv = lax.rsqrt(jnp.mean(cen * cen, axis=-1, keepdims=True) + EPS)
    return cen * inv, inv


def factors(p, m):
    p0, p1, p2, p3 = p
    s1 = jax.nn.sigmoid(p1)
    s3 = jax.nn.sigmoid(p3)
    f0 = m * s1
    f2 = m * s3
    left = f0 * p0
    right = f2 * p2
    return (f0, left * (1.0 - s1), f2, right * (1.0 - s3)), left, right


def kernel(
    nr, nc, nq,
    tok_s, tok_v, pair, pm, gain, wt, gt,
    out, wout,
    normed, fac, lt, rt, lrs, lrr, gfull, dsend, drecv, df, asend, arecv,
    wf, fo, stdo, invo, ag, ws, wr, xr, wg,
    g1_s, g1_r, g2_s, g2_r, wf_s, wf_r, lr_s, lr_r, d_s, d_r, a_s, a_r,
    ag_s, ag_r, wa_s, wa_r, wb_s, wb_r, wc_s, wc_r,
):
    r = lax.axis_index("row")
    c = lax.axis_index("col")
    q = lax.axis_index("ch")
    ni, nk, cc = pair.shape
    hq = wt.shape[0] // 4
    n = nc * ni
    nj = gfull.shape[2]
    t_n = ni // nq
    jpb = nj // ni

    def peer(axis, size, me, off):
        return lax.rem(me + off, size)

    def remote(src, dst, s, rr, axis, to):
        return pltpu.make_async_remote_copy(
            src_ref=src, dst_ref=dst, send_sem=s, recv_sem=rr,
            device_id={axis: to}, device_id_type=MESH,
        )

    barrier = pltpu.get_barrier_semaphore()
    for axis, size, me in (("row", nr, r), ("col", nc, c), ("ch", nq, q)):
        def greet(off, carry, axis=axis, size=size, me=me):
            pl.semaphore_signal(
                barrier, inc=1, device_id={axis: peer(axis, size, me, off)},
                device_id_type=MESH,
            )
            return carry
        lax.fori_loop(1, size, greet, 0)
    pl.semaphore_wait(barrier, nr + nc + nq - 3)

    def spread(size, me, make, start=True):
        def one(off, carry):
            to = lax.rem(me + off, size)
            copy = make(to, to, me)
            if start:
                copy.start()
            else:
                copy.wait_send()
            return carry
        lax.fori_loop(1, size, one, 0)

    def gather(size, me, make):
        def one(off, carry):
            src = lax.rem(me + off, size)
            make(src, src, src).wait_recv()
            return carry
        lax.fori_loop(1, size, one, 0)

    lane = pl.ds(pl.multiple_of(r * nj, nj), nj)

    def rows_of(b):
        return pl.ds(pl.multiple_of(b * ni, ni), ni)

    def g1(to, slot, src):
        return remote(gt.at[slot, :, lane], gfull.at[r, rows_of(src)],
                      g1_s.at[slot], g1_r.at[src], "col", to)

    def g2(to, slot, src):
        return remote(gfull.at[src], gfull.at[src], g2_s.at[slot], g2_r.at[src], "row", to)

    def wfc(to, slot, src):
        return remote(wt, wf.at[src], wf_s.at[slot], wf_r.at[src], "ch", to)

    def lrc(to, slot, src):
        return remote(lrs.at[slot], lrr.at[src], lr_s.at[slot], lr_r.at[src], "col", to)

    def dc(to, slot, src):
        return remote(dsend.at[slot], drecv.at[src], d_s.at[slot], d_r.at[src], "col", to)

    def ac(to, slot, src):
        return remote(asend.at[slot], arecv.at[src], a_s.at[slot], a_r.at[src], "ch", to)

    def wa(to, slot, src):
        return remote(ws.at[slot], wr.at[src], wa_s.at[slot], wa_r.at[src], "col", to)

    def wb(to, slot, src):
        return remote(xr.at[src], xr.at[src], wb_s.at[slot], wb_r.at[src], "row", to)

    def wc(to, slot, src):
        return remote(wg.at[src], wg.at[src], wc_s.at[slot], wc_r.at[src], "col", to)

    spread(nc, c, g1)
    spread(nq, q, wfc)
    gfull[r, rows_of(c)] = gt[c, :, lane]
    wf[q] = wt[...]

    tok_k = tok_v[pl.ds(r, 1), :]
    gain_v = gain[...]

    def mask_of(i):
        return (pm[pl.ds(i, 1), :] * tok_k * tok_s[c * ni + i]).astype(F32)

    def project(i, carry):
        std, _ = normalise(pair[i].astype(F32))
        nb = (std * gain_v).astype(BF16)
        normed[i] = nb
        p = lax.dot_general(wt[...], nb, NT, preferred_element_type=F32)
        p = p.reshape(4, hq, nk)
        f, left, right = factors((p[0], p[1], p[2], p[3]), mask_of(i))
        for g in range(4):
            fac[i, g] = f[g]
        lt[i] = left
        rt[i] = right
        return carry

    lax.fori_loop(0, ni, project, 0, unroll=4)

    for h in range(hq):
        lrs[h, 0] = lt[:, h, :].astype(BF16)
        lrs[h, 1] = rt[:, h, :].astype(BF16)
    spread(nc, c, lrc)
    lrr[c] = lrs[c]

    gather(nc, c, g1)
    spread(nr, r, g2)

    gather(nq, q, wfc)

    def own(t, carry):
        i = q * t_n + t
        std, inv = normalise(pair[i].astype(F32))
        stdo[t] = std
        invo[t] = jnp.broadcast_to(inv, (nk, cc))
        p = lax.dot_general(wf[...].reshape(nq * 4 * hq, cc), normed[i], NT,
                            preferred_element_type=F32)
        p = p.reshape(nq, 4, hq, nk)
        f, _, _ = factors((p[:, 0], p[:, 1], p[:, 2], p[:, 3]), mask_of(i))
        for g in range(4):
            fo[t, g] = f[g]
        return carry

    lax.fori_loop(0, t_n, own, 0)

    gather(nr, r, g2)
    gather(nc, c, lrc)

    left_all = lrr[:, 0].reshape(n, nk)
    dl = jnp.zeros((n, nk), F32)
    for x in range(nr):
        rx = lrr[x * jpb:(x + 1) * jpb, 1].reshape(nj, nk)
        dl = dl + jnp.dot(gfull[x], rx, preferred_element_type=F32)
        dr = lax.dot_general(gfull[x], left_all, TN, preferred_element_type=F32)
        dsend[x * jpb:(x + 1) * jpb, 1] = dr.astype(BF16).reshape(jpb, ni, nk)
    dsend[:, 0] = dl.astype(BF16).reshape(nc, ni, nk)
    spread(nc, c, dc)
    drecv[c] = dsend[c]
    gather(nc, c, dc)

    for side in range(2):
        df[side] = drecv[:, side].astype(F32)
    for b in range(nq):
        for t in range(t_n):
            for side in range(2):
                asend[b, side, t] = df[side, :, b * t_n + t, :].astype(BF16)
    spread(nq, q, ac)
    arecv[q] = asend[q]

    def weigh(i, acc):
        b = i // t_n
        t = i - b * t_n
        d0 = asend[b, 0, t].astype(F32)
        d1 = asend[b, 1, t].astype(F32)
        f = fac[i]
        gr = jnp.concatenate([d0 * f[0], d0 * f[1], d1 * f[2], d1 * f[3]], axis=0).astype(BF16)
        return acc + jnp.dot(gr, normed[i], preferred_element_type=F32)

    w_part = lax.fori_loop(0, ni, weigh, jnp.zeros((4 * hq, cc), F32), unroll=4)
    wrows = 4 * hq // nc
    for b in range(nc):
        ws[b] = jnp.concatenate(
            [w_part[b * wrows:(b + 1) * wrows], jnp.zeros((8 - wrows, cc), F32)], axis=0)
    spread(nc, c, wa)
    wr[c] = ws[c]

    gather(nq, q, ac)

    def to_right(b, t):
        return remote(ag.at[b, t], ag.at[b, t], ag_s.at[0, b, t], ag_r.at[b, t], "ch",
                      lax.rem(q + 1, nq))

    def to_left(b, t):
        return remote(ag.at[b, t], ag.at[b, t], ag_s.at[1, b, t], ag_r.at[b, t], "ch",
                      lax.rem(q + nq - 1, nq))

    def back(t, carry):
        d0 = arecv[:, 0, t].astype(F32)
        d1 = arecv[:, 1, t].astype(F32)
        f = fo[t]
        gr = jnp.stack([d0 * f[0], d0 * f[1], d1 * f[2], d1 * f[3]], axis=1).astype(BF16)
        d_norm = lax.dot_general(gr.reshape(nq * 4 * hq, nk), wf[...].reshape(nq * 4 * hq, cc),
                                 TN, preferred_element_type=F32)
        e = d_norm * gain_v
        std = stdo[t]
        first = jnp.mean(e, axis=-1, keepdims=True)
        second = jnp.mean(e * std, axis=-1, keepdims=True)
        ag[q, t] = (invo[t] * (e - first - std * second)).astype(BF16)

        @pl.when(q < nq - 1)
        def _():
            to_right(q, t).start()

        @pl.when(q > 0)
        def _():
            to_left(q, t).start()
        return carry

    lax.fori_loop(0, t_n, back, 0)

    def relay(s):
        def one(t, carry):
            @pl.when(q >= s)
            def _():
                to_right(q - s, t).wait_recv()

                @pl.when(q < nq - 1)
                def _():
                    to_right(q - s, t).start()

            @pl.when(q + s < nq)
            def _():
                to_left(q + s, t).wait_recv()

                @pl.when(q > 0)
                def _():
                    to_left(q + s, t).start()
            return carry
        lax.fori_loop(0, t_n, one, 0)

    gather(nc, c, wa)
    xr[r] = jnp.sum(wr[...], axis=0)
    spread(nr, r, wb)
    relay(1)
    gather(nr, r, wb)
    total = xr[0]
    for x in range(1, nr):
        total = total + xr[x]
    wg[c] = total * (1.0 / n)
    spread(nc, c, wc)
    for s in range(2, nq):
        relay(s)
    gather(nc, c, wc)
    for b in range(nc):
        wout[b * wrows:(b + 1) * wrows, :] = wg[b, :wrows, :]
    out[...] = ag[...].reshape(ni, nk, cc)

    spread(nc, c, g1, False)
    spread(nq, q, wfc, False)
    spread(nc, c, lrc, False)
    spread(nr, r, g2, False)
    spread(nc, c, dc, False)
    spread(nq, q, ac, False)
    spread(nc, c, wa, False)
    spread(nr, r, wb, False)
    spread(nc, c, wc, False)

    def drain(b, carry):
        def one(t, carry):
            @pl.when(jnp.logical_and(b <= q, q < nq - 1))
            def _():
                to_right(b, t).wait_send()

            @pl.when(jnp.logical_and(b >= q, q > 0))
            def _():
                to_left(b, t).wait_send()
            return carry
        return lax.fori_loop(0, t_n, one, carry)
    lax.fori_loop(0, nq, drain, 0)


def body(nr, nc, nq, pair, token_mask, pair_mask, ln_gain, w_in, grad_tri):
    ni, nk, cc = pair.shape
    hq = w_in.shape[2]
    n = nc * ni
    nj = n // nr
    t_n = ni // nq
    wt = jnp.transpose(w_in, (1, 2, 0)).reshape(4 * hq, cc)
    vmem = pl.BlockSpec(memory_space=pltpu.VMEM)
    smem = pl.BlockSpec(memory_space=pltpu.SMEM)
    dma = lambda *s: pltpu.SemaphoreType.DMA(s)
    out, wout = pl.pallas_call(
        functools.partial(kernel, nr, nc, nq),
        out_shape=(
            jax.ShapeDtypeStruct((ni, nk, cc), BF16),
            jax.ShapeDtypeStruct((4 * hq, cc), F32),
        ),
        in_specs=[smem] + [vmem] * 6,
        out_specs=(vmem, vmem),
        scratch_shapes=[
            pltpu.VMEM((ni, nk, cc), BF16),
            pltpu.VMEM((ni, 4, hq, nk), F32),
            pltpu.VMEM((ni, hq, nk), F32),
            pltpu.VMEM((ni, hq, nk), F32),
            pltpu.VMEM((nc, 2, ni, nk), BF16),
            pltpu.VMEM((nc, 2, ni, nk), BF16),
            pltpu.VMEM((nr, n, nj), BF16),
            pltpu.VMEM((nc, 2, ni, nk), BF16),
            pltpu.VMEM((nc, 2, ni, nk), BF16),
            pltpu.VMEM((2, hq, ni, nk), F32),
            pltpu.VMEM((nq, 2, t_n, hq, nk), BF16),
            pltpu.VMEM((nq, 2, t_n, hq, nk), BF16),
            pltpu.VMEM((nq, 4 * hq, cc), BF16),
            pltpu.VMEM((t_n, 4, nq, hq, nk), F32),
            pltpu.VMEM((t_n, nk, cc), F32),
            pltpu.VMEM((t_n, nk, cc), F32),
            pltpu.VMEM((nq, t_n, nk, cc), BF16),
            pltpu.VMEM((nc, 8, cc), F32),
            pltpu.VMEM((nc, 8, cc), F32),
            pltpu.VMEM((nr, 8, cc), F32),
            pltpu.VMEM((nc, 8, cc), F32),
            dma(nc), dma(nc), dma(nr), dma(nr), dma(nq), dma(nq),
            dma(nc), dma(nc), dma(nc), dma(nc), dma(nq), dma(nq),
            dma(2, nq, t_n), dma(nq, t_n),
            dma(nc), dma(nc), dma(nr), dma(nr), dma(nc), dma(nc),
        ],
        compiler_params=pltpu.CompilerParams(
            collective_id=0, has_side_effects=True, vmem_limit_bytes=48 * 1024 * 1024,
        ),
        name="triangle_backward",
    )(token_mask, token_mask.reshape(nr, nk), pair, pair_mask, ln_gain.reshape(1, cc), wt, grad_tri)
    w_grad = jnp.transpose(wout.reshape(4, hq, cc), (2, 0, 1))
    return out, w_grad


def solution(mesh):
    size = dict(mesh.shape)
    return jax.shard_map(
        functools.partial(body, size["row"], size["col"], size["ch"]),
        mesh=mesh,
        in_specs=(
            P("col", "row", None),
            P(),
            P("col", "row"),
            P(),
            P(None, None, "ch"),
            P("ch", "col", None),
        ),
        out_specs=(P("col", "row", None), P(None, None, "ch")),
        check_vma=False,
    )
```

```python
import functools

import jax
import jax.numpy as jnp
from jax import lax
from jax.experimental import pallas as pl
from jax.experimental.pallas import tpu as pltpu
from jax.sharding import PartitionSpec as P

EPS = 1e-05
F32 = jnp.float32
BF16 = jnp.bfloat16
MESH = pl.DeviceIdType.MESH
NT = (((1,), (1,)), ((), ()))
TN = (((0,), (0,)), ((), ()))


def normalise(x):
    mean = jnp.mean(x, axis=-1, keepdims=True)
    cen = x - mean
    inv = lax.rsqrt(jnp.mean(cen * cen, axis=-1, keepdims=True) + EPS)
    return cen * inv, inv


def factors(p, m):
    p0, p1, p2, p3 = p
    s1 = jax.nn.sigmoid(p1)
    s3 = jax.nn.sigmoid(p3)
    f0 = m * s1
    f2 = m * s3
    return f0, f0 * p0 * (1.0 - s1), f2, f2 * p2 * (1.0 - s3)


def kernel(
    nr, nc, nq,
    tok, pair_h, pm_h, gain_h, w_h, gt,
    out, wout,
    tok_v, pair, pm, gain, w_v, mask, wt,
    normed, lt, rt, lrs, lrr, gfull, dsend, drecv, df, asend, arecv,
    wf, fo, stdo, invo, gro, ag, wp, wr, zp, zr, xr, wg,
    in_s, o_s,
    g1_s, g1_r, g2_s, g2_r, wf_s, wf_r, lr_s, lr_r, d_s, d_r, a_s, a_r,
    ag_s, ag_r, wa_s, wa_r, wb_s, wb_r, wc_s, wc_r, wd_s, wd_r,
):
    r = lax.axis_index("row")
    c = lax.axis_index("col")
    q = lax.axis_index("ch")
    ni, nk, cc = pair.shape
    hq = nc
    n = nc * ni
    nj = gfull.shape[2]
    t_n = ni // nq
    jpb = nj // ni
    npl = nc // 2
    nz = 2 * nq
    zh = lax.rem(lax.div(c, 2), 2)
    m = lax.div(c, 4) * 2 + lax.rem(c, 2)
    z = zh * nq + q

    def col_of(zh_, m_):
        return (lax.div(m_, 2) * 2 + zh_) * 2 + lax.rem(m_, 2)

    def pos(c_):
        return lax.rem(lax.div(c_, 2), 2) * npl + lax.div(c_, 4) * 2 + lax.rem(c_, 2)

    def to_row(i):
        return {"row": i}

    def to_col(i):
        return {"col": i}

    def to_ch(i):
        return {"ch": i}

    def to_plane(i):
        return {"col": col_of(zh, i)}

    def to_z(i):
        return {"col": col_of(lax.div(i, nq), m), "ch": lax.rem(i, nq)}

    loads = [
        pltpu.make_async_copy(src, dst, in_s.at[k])
        for k, (src, dst) in enumerate(
            ((w_h, w_v), (tok, tok_v), (pm_h, pm), (gain_h, gain), (pair_h, pair)))
    ]
    for load in loads:
        load.start()

    barrier = pltpu.get_barrier_semaphore()

    def greet(device):
        pl.semaphore_signal(barrier, inc=1, device_id=device, device_id_type=MESH)

    def greet_all(size, me, to):
        def one(off, carry):
            greet(to(lax.rem(me + off, size)))
            return carry
        lax.fori_loop(1, size, one, 0)

    greet_all(nr, r, to_row)
    greet_all(nc, c, to_col)
    greet_all(nq, q, to_ch)

    def greet_far(off, carry):
        greet({"col": col_of(1 - zh, m), "ch": lax.rem(q + off, nq)})
        return carry
    lax.fori_loop(1, nq, greet_far, 0)

    for load in loads:
        load.wait()

    def permuted(w):
        rows = []
        for g in range(4):
            for half in range(2):
                for y in range(nc // 4):
                    at = g * hq + (y * 2 + half) * 2
                    rows.append(w[at:at + 2])
        return jnp.concatenate(rows, axis=0)

    def natural(w):
        rows = []
        for g in range(4):
            for y in range(nc // 4):
                for half in range(2):
                    at = g * hq + half * npl + y * 2
                    rows.append(w[at:at + 2])
        return jnp.concatenate(rows, axis=0)

    wv = permuted(w_v[...].astype(F32)).astype(BF16)
    wt[...] = wv
    wf[q] = wv

    tok_k = tok_v[pl.ds(r, 1), :]
    first = c * ni
    tok_i = tok_v[pl.ds(lax.div(first, nk), 1), :]
    at = lax.broadcasted_iota(jnp.int32, (ni, nk), 1) - lax.rem(first, nk)
    hit = at == lax.broadcasted_iota(jnp.int32, (ni, nk), 0)
    tok_i = jnp.sum(jnp.where(hit, tok_i, 0).astype(F32), axis=1, keepdims=True)
    mask[...] = (pm[...] * tok_k).astype(F32) * tok_i
    gain_v = gain[...]

    pl.semaphore_wait(barrier, nr + nc + 2 * nq - 4)

    def remote(src, dst, s, rr, device):
        return pltpu.make_async_remote_copy(
            src_ref=src, dst_ref=dst, send_sem=s, recv_sem=rr,
            device_id=device, device_id_type=MESH,
        )

    def spread(size, me, make, start=True):
        def one(off, carry):
            to = lax.rem(me + off, size)
            copy = make(to, me)
            if start:
                copy.start()
            else:
                copy.wait_send()
            return carry
        lax.fori_loop(1, size, one, 0)

    def gather(size, me, make):
        def one(off, carry):
            src = lax.rem(me + off, size)
            make(src, src).wait_recv()
            return carry
        lax.fori_loop(1, size, one, 0)

    lane = pl.ds(pl.multiple_of(r * nj, nj), nj)

    def rows_of(b):
        return pl.ds(pl.multiple_of(b * ni, ni), ni)

    def g1(to, src):
        return remote(gt.at[to, :, lane], gfull.at[r, rows_of(src)],
                      g1_s.at[to], g1_r.at[src], to_col(to))

    def g2(to, src):
        return remote(gfull.at[src], gfull.at[src], g2_s.at[to], g2_r.at[src], to_row(to))

    def wfc(to, src):
        return remote(wt, wf.at[src], wf_s.at[to], wf_r.at[src], to_ch(to))

    def lrc(to, src):
        return remote(lrs.at[pos(to)], lrr.at[src], lr_s.at[to], lr_r.at[src], to_col(to))

    def dc(to, src):
        return remote(dsend.at[to], drecv.at[src], d_s.at[to], d_r.at[src], to_plane(to))

    def ac(to, src):
        return remote(asend.at[to], arecv.at[src], a_s.at[to], a_r.at[src], to_z(to))

    def wa(to, src):
        return remote(wp.at[to], wr.at[src], wa_s.at[to], wa_r.at[src], to_plane(to))

    def wb(to, src):
        return remote(zp.at[lax.rem(to, nq)], zr.at[src], wb_s.at[to], wb_r.at[src], to_z(to))

    def wc(to, src):
        return remote(xr.at[src], xr.at[src], wc_s.at[to], wc_r.at[src], to_row(to))

    def wd(to, src):
        return remote(wg.at[src], wg.at[src], wd_s.at[to], wd_r.at[src], to_plane(to))

    spread(nc, c, g1)
    spread(nq, q, wfc)
    mine = pltpu.make_async_copy(gt.at[c, :, lane], gfull.at[r, rows_of(c)], g1_s.at[c])
    mine.start()

    def mask_of(i):
        return mask[pl.ds(i, 1), :]

    def project(i, carry):
        std, _ = normalise(pair[i].astype(F32))
        nb = (std * gain_v).astype(BF16)
        normed[i] = nb
        p = lax.dot_general(wt[...], nb, NT, preferred_element_type=F32)
        p = p.reshape(4, hq, nk)
        mk = mask_of(i)
        lt[i] = mk * jax.nn.sigmoid(p[1]) * p[0]
        rt[i] = mk * jax.nn.sigmoid(p[3]) * p[2]
        return carry

    lax.fori_loop(0, ni, project, 0, unroll=4)

    for h in range(hq):
        lrs[h, 0] = lt[:, h, :].astype(BF16)
        lrs[h, 1] = rt[:, h, :].astype(BF16)
    spread(nc, c, lrc)
    lrr[c] = lrs[pos(c)]

    gather(nq, q, wfc)

    def own(t, carry):
        i = q * t_n + t
        std, inv = normalise(pair[i].astype(F32))
        stdo[t] = std
        invo[t] = jnp.broadcast_to(inv, (nk, cc))
        p = lax.dot_general(wf[...].reshape(nq * 4 * hq, cc), normed[i], NT,
                            preferred_element_type=F32)
        p = p.reshape(nq, 4, hq, nk)
        f = factors((p[:, 0], p[:, 1], p[:, 2], p[:, 3]), mask_of(i))
        for g in range(4):
            fo[t, g] = f[g]
        return carry

    lax.fori_loop(0, t_n, own, 0)

    gather(nc, c, g1)
    mine.wait()
    spread(nr, r, g2)
    gather(nr, r, g2)
    gather(nc, c, lrc)

    left_all = lrr[:, 0].reshape(n, nk)
    dl = jnp.zeros((n, nk), F32)
    for x in range(nr):
        rx = lrr[x * jpb:(x + 1) * jpb, 1].reshape(nj, nk)
        dl = dl + jnp.dot(gfull[x], rx, preferred_element_type=F32)
        dr = lax.dot_general(gfull[x], left_all, TN, preferred_element_type=F32)
        dr = dr.astype(BF16).reshape(jpb, ni, nk)
        for b in range(jpb):
            cb = x * jpb + b
            dsend[cb // 4 * 2 + cb % 2, cb // 2 % 2, 1] = dr[b]
    dl = dl.astype(BF16).reshape(nc, ni, nk)
    for cb in range(nc):
        dsend[cb // 4 * 2 + cb % 2, cb // 2 % 2, 0] = dl[cb]
    spread(npl, m, dc)
    drecv[m] = dsend[m]
    gather(npl, m, dc)

    for half in range(2):
        for side in range(2):
            df[half, side] = drecv[:, half, side].astype(F32)
    for half in range(2):
        for b in range(nq):
            for t in range(t_n):
                i = b * t_n + t
                asend[half * nq + b, t] = jnp.concatenate(
                    [df[half, 0, :, i, :], df[half, 1, :, i, :]], axis=0).astype(BF16)
    spread(nz, z, ac)
    arecv[z] = asend[z]
    gather(nz, z, ac)

    def to_right(b, t):
        return remote(ag.at[b, t], ag.at[b, t], ag_s.at[0, b, t], ag_r.at[b, t],
                      to_ch(lax.rem(q + 1, nq)))

    def to_left(b, t):
        return remote(ag.at[b, t], ag.at[b, t], ag_s.at[1, b, t], ag_r.at[b, t],
                      to_ch(lax.rem(q + nq - 1, nq)))

    def keep(b, t):
        return pltpu.make_async_copy(ag.at[b, t], out.at[b * t_n + t], o_s.at[b, t])

    for t in range(t_n):
        d = jnp.stack([
            jnp.stack([arecv[half * nq + b, t].astype(F32) for half in range(2)])
            for b in range(nq)])
        d0 = d[:, :, :npl].reshape(nq, hq, nk)
        d1 = d[:, :, npl:].reshape(nq, hq, nk)
        f = fo[t]
        gr = jnp.stack([d0 * f[0], d0 * f[1], d1 * f[2], d1 * f[3]], axis=1)
        gr = gr.reshape(nq * 4 * hq, nk).astype(BF16)
        gro[:, t * nk:(t + 1) * nk] = gr
        d_norm = lax.dot_general(gr, wf[...].reshape(nq * 4 * hq, cc),
                                 TN, preferred_element_type=F32)
        e = d_norm * gain_v
        std = stdo[t]
        first = jnp.mean(e, axis=-1, keepdims=True)
        second = jnp.mean(e * std, axis=-1, keepdims=True)
        ag[q, t] = (invo[t] * (e - first - std * second)).astype(BF16)
        keep(q, t).start()

        @pl.when(q < nq - 1)
        def _():
            to_right(q, t).start()

        @pl.when(q > 0)
        def _():
            to_left(q, t).start()

    nb = normed[pl.ds(q * t_n, t_n)].reshape(t_n * nk, cc)
    w_part = jnp.dot(gro[...], nb, preferred_element_type=F32).reshape(nq, npl, 8, cc)
    for b in range(npl):
        wp[b] = w_part[:, b]
    spread(npl, m, wa)
    wr[m] = wp[m]

    def relay(s):
        def one(t, carry):
            @pl.when(q >= s)
            def _():
                to_right(q - s, t).wait_recv()

                @pl.when(q < nq - 1)
                def _():
                    to_right(q - s, t).start()
                keep(q - s, t).start()

            @pl.when(q + s < nq)
            def _():
                to_left(q + s, t).wait_recv()

                @pl.when(q > 0)
                def _():
                    to_left(q + s, t).start()
                keep(q + s, t).start()
            return carry
        lax.fori_loop(0, t_n, one, 0)

    relay(1)
    gather(npl, m, wa)
    zp[...] = jnp.sum(wr[...], axis=0)
    spread(nz, z, wb)
    zr[z] = zp[q]
    for s in range(2, max(3, nq - 3)):
        if s < nq:
            relay(s)
    gather(nz, z, wb)
    xr[r] = jnp.sum(zr[...], axis=0)
    spread(nr, r, wc)
    for s in range(max(3, nq - 3), nq - 1):
        relay(s)
    gather(nr, r, wc)
    total = xr[0]
    for x in range(1, nr):
        total = total + xr[x]
    wg[m] = total * (1.0 / n)
    spread(npl, m, wd)
    if nq - 1 >= max(3, nq - 3):
        relay(nq - 1)
    gather(npl, m, wd)
    wout[...] = natural(wg[...].reshape(4 * hq, cc))

    spread(nc, c, g1, False)
    spread(nq, q, wfc, False)
    spread(nc, c, lrc, False)
    spread(nr, r, g2, False)
    spread(npl, m, dc, False)
    spread(nz, z, ac, False)
    spread(npl, m, wa, False)
    spread(nz, z, wb, False)
    spread(nr, r, wc, False)
    spread(npl, m, wd, False)

    def drain(b, carry):
        def one(t, carry):
            @pl.when(jnp.logical_and(b <= q, q < nq - 1))
            def _():
                to_right(b, t).wait_send()

            @pl.when(jnp.logical_and(b >= q, q > 0))
            def _():
                to_left(b, t).wait_send()
            keep(b, t).wait()
            return carry
        return lax.fori_loop(0, t_n, one, carry)
    lax.fori_loop(0, nq, drain, 0)


def body(nr, nc, nq, pair, token_mask, pair_mask, ln_gain, w_in, grad_tri):
    ni, nk, cc = pair.shape
    hq = w_in.shape[2]
    n = nc * ni
    nj = n // nr
    t_n = ni // nq
    npl = nc // 2
    nz = 2 * nq
    wt = jnp.transpose(w_in, (1, 2, 0)).reshape(4 * hq, cc)
    vmem = pl.BlockSpec(memory_space=pltpu.VMEM)
    hbm = pl.BlockSpec(memory_space=pltpu.HBM)
    dma = lambda *s: pltpu.SemaphoreType.DMA(s)
    out, wout = pl.pallas_call(
        functools.partial(kernel, nr, nc, nq),
        out_shape=(
            jax.ShapeDtypeStruct((ni, nk, cc), BF16),
            jax.ShapeDtypeStruct((4 * hq, cc), F32),
        ),
        in_specs=[hbm] * 6,
        out_specs=(hbm, vmem),
        scratch_shapes=[
            pltpu.VMEM((n // nk, nk), jnp.int32),
            pltpu.VMEM((ni, nk, cc), BF16),
            pltpu.VMEM((ni, nk), jnp.int32),
            pltpu.VMEM((1, cc), F32),
            pltpu.VMEM((4 * hq, cc), BF16),
            pltpu.VMEM((ni, nk), F32),
            pltpu.VMEM((4 * hq, cc), BF16),
            pltpu.VMEM((ni, nk, cc), BF16),
            pltpu.VMEM((ni, hq, nk), F32),
            pltpu.VMEM((ni, hq, nk), F32),
            pltpu.VMEM((nc, 2, ni, nk), BF16),
            pltpu.VMEM((nc, 2, ni, nk), BF16),
            pltpu.VMEM((nr, n, nj), BF16),
            pltpu.VMEM((npl, 2, 2, ni, nk), BF16),
            pltpu.VMEM((npl, 2, 2, ni, nk), BF16),
            pltpu.VMEM((2, 2, npl, ni, nk), F32),
            pltpu.VMEM((nz, t_n, hq, nk), BF16),
            pltpu.VMEM((nz, t_n, hq, nk), BF16),
            pltpu.VMEM((nq, 4 * hq, cc), BF16),
            pltpu.VMEM((t_n, 4, nq, hq, nk), F32),
            pltpu.VMEM((t_n, nk, cc), F32),
            pltpu.VMEM((t_n, nk, cc), F32),
            pltpu.VMEM((nq * 4 * hq, t_n * nk), BF16),
            pltpu.VMEM((nq, t_n, nk, cc), BF16),
            pltpu.VMEM((npl, nq, 8, cc), F32),
            pltpu.VMEM((npl, nq, 8, cc), F32),
            pltpu.VMEM((nq, 8, cc), F32),
            pltpu.VMEM((nz, 8, cc), F32),
            pltpu.VMEM((nr, 8, cc), F32),
            pltpu.VMEM((npl, 8, cc), F32),
            dma(5), dma(nq, t_n),
            dma(nc), dma(nc), dma(nr), dma(nr), dma(nq), dma(nq),
            dma(nc), dma(nc), dma(npl), dma(npl), dma(nz), dma(nz),
            dma(2, nq, t_n), dma(nq, t_n),
            dma(npl), dma(npl), dma(nz), dma(nz), dma(nr), dma(nr), dma(npl), dma(npl),
        ],
        compiler_params=pltpu.CompilerParams(
            collective_id=0, has_side_effects=True, vmem_limit_bytes=48 * 1024 * 1024,
        ),
        name="triangle_backward",
    )(token_mask.reshape(n // nk, nk), pair, pair_mask, ln_gain.reshape(1, cc), wt, grad_tri)
    w_grad = jnp.transpose(wout.reshape(4, hq, cc), (2, 0, 1))
    return out, w_grad


def solution(mesh):
    size = dict(mesh.shape)
    return jax.shard_map(
        functools.partial(body, size["row"], size["col"], size["ch"]),
        mesh=mesh,
        in_specs=(
            P("col", "row", None),
            P(),
            P("col", "row"),
            P(),
            P(None, None, "ch"),
            P("ch", "col", None),
        ),
        out_specs=(P("col", "row", None), P(None, None, "ch")),
        check_vma=False,
    )
```

```python
import functools

import jax
import jax.numpy as jnp
from jax import lax
from jax.experimental import pallas as pl
from jax.experimental.pallas import tpu as pltpu
from jax.sharding import PartitionSpec as P

EPS = 1e-05
F32 = jnp.float32
BF16 = jnp.bfloat16
MESH = pl.DeviceIdType.MESH
NT = (((1,), (1,)), ((), ()))
TN = (((0,), (0,)), ((), ()))


def normalise(x):
    mean = jnp.mean(x, axis=-1, keepdims=True)
    cen = x - mean
    inv = lax.rsqrt(jnp.mean(cen * cen, axis=-1, keepdims=True) + EPS)
    return cen * inv, inv


def factors(p, m):
    p0, p1, p2, p3 = p
    s1 = jax.nn.sigmoid(p1)
    s3 = jax.nn.sigmoid(p3)
    f0 = m * s1
    f2 = m * s3
    return f0, f0 * p0 * (1.0 - s1), f2, f2 * p2 * (1.0 - s3)


def kernel(
    nr, nc, nq,
    tok, pair_h, pm_h, gain_h, w_h, gt,
    out, wout,
    tok_v, pair, pm, gain, w_v, mask, wt,
    normed, lt, rt, lrs, lrr, gfull, dsend, drecv, df, asend, arecv,
    wf, fo, stdo, invo, gro, ag, wp, wr, zp, zq, zr, xr, wg,
    in_s, o_s,
    g1_s, g1_r, g2_s, g2_r, wf_s, wf_r, lr_s, lr_r, d_s, d_r, a_s, a_r,
    ag_s, ag_r, wa_s, wa_r, wx_s, wx_r, wz_s, wz_r, wb_s, wb_r, wd_s, wd_r,
):
    r = lax.axis_index("row")
    c = lax.axis_index("col")
    q = lax.axis_index("ch")
    ni, nk, cc = pair.shape
    hq = nc
    n = nc * ni
    nj = gfull.shape[2]
    t_n = ni // nq
    jpb = nj // ni
    npl = nc // 2
    nz = 2 * nq
    zh = lax.rem(lax.div(c, 2), 2)
    m = lax.div(c, 4) * 2 + lax.rem(c, 2)
    z = zh * nq + q

    def col_of(zh_, m_):
        return (lax.div(m_, 2) * 2 + zh_) * 2 + lax.rem(m_, 2)

    def pos(c_):
        return lax.rem(lax.div(c_, 2), 2) * npl + lax.div(c_, 4) * 2 + lax.rem(c_, 2)

    def to_row(i):
        return {"row": i}

    def to_col(i):
        return {"col": i}

    def to_ch(i):
        return {"ch": i}

    def to_plane(i):
        return {"col": col_of(zh, i)}

    def to_z(i):
        return {"col": col_of(lax.div(i, nq), m), "ch": lax.rem(i, nq)}

    loads = [
        pltpu.make_async_copy(src, dst, in_s.at[k])
        for k, (src, dst) in enumerate(
            ((w_h, w_v), (tok, tok_v), (pm_h, pm), (gain_h, gain), (pair_h, pair)))
    ]
    for load in loads:
        load.start()

    barrier = pltpu.get_barrier_semaphore()

    def greet(device):
        pl.semaphore_signal(barrier, inc=1, device_id=device, device_id_type=MESH)

    def greet_all(size, me, to):
        def one(off, carry):
            greet(to(lax.rem(me + off, size)))
            return carry
        lax.fori_loop(1, size, one, 0)

    greet_all(nr, r, to_row)
    greet_all(nc, c, to_col)
    greet_all(nq, q, to_ch)

    def greet_far(off, carry):
        greet({"col": col_of(1 - zh, m), "ch": lax.rem(q + off, nq)})
        return carry
    lax.fori_loop(1, nq, greet_far, 0)

    for load in loads:
        load.wait()

    def permuted(w):
        rows = []
        for g in range(4):
            for half in range(2):
                for y in range(nc // 4):
                    at = g * hq + (y * 2 + half) * 2
                    rows.append(w[at:at + 2])
        return jnp.concatenate(rows, axis=0)

    def natural(w):
        rows = []
        for g in range(4):
            for y in range(nc // 4):
                for half in range(2):
                    at = g * hq + half * npl + y * 2
                    rows.append(w[at:at + 2])
        return jnp.concatenate(rows, axis=0)

    wv = permuted(w_v[...].astype(F32)).astype(BF16)
    wt[...] = wv
    wf[q] = wv

    tok_k = tok_v[pl.ds(r, 1), :]
    first = c * ni
    tok_i = tok_v[pl.ds(lax.div(first, nk), 1), :]
    at = lax.broadcasted_iota(jnp.int32, (ni, nk), 1) - lax.rem(first, nk)
    hit = at == lax.broadcasted_iota(jnp.int32, (ni, nk), 0)
    tok_i = jnp.sum(jnp.where(hit, tok_i, 0).astype(F32), axis=1, keepdims=True)
    mask[...] = (pm[...] * tok_k).astype(F32) * tok_i
    gain_v = gain[...]

    pl.semaphore_wait(barrier, nr + nc + 2 * nq - 4)

    def remote(src, dst, s, rr, device):
        return pltpu.make_async_remote_copy(
            src_ref=src, dst_ref=dst, send_sem=s, recv_sem=rr,
            device_id=device, device_id_type=MESH,
        )

    def spread(size, me, make, start=True):
        def one(off, carry):
            to = lax.rem(me + off, size)
            copy = make(to, me)
            if start:
                copy.start()
            else:
                copy.wait_send()
            return carry
        lax.fori_loop(1, size, one, 0)

    def gather(size, me, make):
        def one(off, carry):
            src = lax.rem(me + off, size)
            make(src, src).wait_recv()
            return carry
        lax.fori_loop(1, size, one, 0)

    lane = pl.ds(pl.multiple_of(r * nj, nj), nj)

    def rows_of(b):
        return pl.ds(pl.multiple_of(b * ni, ni), ni)

    def g1(to, src):
        return remote(gt.at[to, :, lane], gfull.at[r, rows_of(src)],
                      g1_s.at[to], g1_r.at[src], to_col(to))

    def g2(to, src):
        return remote(gfull.at[src], gfull.at[src], g2_s.at[to], g2_r.at[src], to_row(to))

    def wfc(to, src):
        return remote(wt, wf.at[src], wf_s.at[to], wf_r.at[src], to_ch(to))

    def lrc(to, src):
        return remote(lrs.at[pos(to)], lrr.at[src], lr_s.at[to], lr_r.at[src], to_col(to))

    def dc(to, src):
        return remote(dsend.at[to], drecv.at[src], d_s.at[to], d_r.at[src], to_plane(to))

    def ac(to, src):
        return remote(asend.at[to], arecv.at[src], a_s.at[to], a_r.at[src], to_z(to))

    def wa(to, src):
        return remote(wp.at[to], wr.at[src], wa_s.at[to], wa_r.at[src], to_plane(to))

    qr = nq // nr
    owner = lax.div(q, qr) == r

    def wx(to, src):
        return remote(zp.at[pl.ds(to * qr, qr)], xr.at[src], wx_s.at[to], wx_r.at[src],
                      to_row(to))

    def wz(half, a):
        to = half * nq + r * qr + a
        return to, remote(zq.at[a], zr.at[z], wz_s.at[half, a], wz_r.at[z], to_z(to))

    def wz_from(to, src):
        return remote(zq.at[0], zr.at[src], wz_s.at[0, 0], wz_r.at[src], to_z(to))

    def wb(to, src):
        return remote(wg.at[m], wg.at[m], wb_s.at[to], wb_r.at[0], to_row(to))

    def wd(to, src):
        return remote(wg.at[src], wg.at[src], wd_s.at[to], wd_r.at[src], to_plane(to))

    spread(nc, c, g1)
    spread(nq, q, wfc)
    mine = pltpu.make_async_copy(gt.at[c, :, lane], gfull.at[r, rows_of(c)], g1_s.at[c])
    mine.start()

    def mask_of(i):
        return mask[pl.ds(i, 1), :]

    def project(i, carry):
        std, _ = normalise(pair[i].astype(F32))
        nb = (std * gain_v).astype(BF16)
        normed[i] = nb
        p = lax.dot_general(wt[...], nb, NT, preferred_element_type=F32)
        p = p.reshape(4, hq, nk)
        mk = mask_of(i)
        lt[i] = mk * jax.nn.sigmoid(p[1]) * p[0]
        rt[i] = mk * jax.nn.sigmoid(p[3]) * p[2]
        return carry

    lax.fori_loop(0, ni, project, 0, unroll=4)

    for h in range(hq):
        lrs[h, 0] = lt[:, h, :].astype(BF16)
        lrs[h, 1] = rt[:, h, :].astype(BF16)
    spread(nc, c, lrc)
    lrr[c] = lrs[pos(c)]

    gather(nc, c, g1)
    mine.wait()
    spread(nr, r, g2)

    gather(nq, q, wfc)

    def own(t, carry):
        i = q * t_n + t
        std, inv = normalise(pair[i].astype(F32))
        stdo[t] = std
        invo[t] = jnp.broadcast_to(inv, (nk, cc))
        p = lax.dot_general(wf[...].reshape(nq * 4 * hq, cc), normed[i], NT,
                            preferred_element_type=F32)
        p = p.reshape(nq, 4, hq, nk)
        f = factors((p[:, 0], p[:, 1], p[:, 2], p[:, 3]), mask_of(i))
        for g in range(4):
            fo[t, g] = f[g]
        return carry

    lax.fori_loop(0, t_n, own, 0)

    gather(nr, r, g2)
    gather(nc, c, lrc)

    left_all = lrr[:, 0].reshape(n, nk)
    dl = jnp.zeros((n, nk), F32)
    for x in range(nr):
        rx = lrr[x * jpb:(x + 1) * jpb, 1].reshape(nj, nk)
        dl = dl + jnp.dot(gfull[x], rx, preferred_element_type=F32)
        dr = lax.dot_general(gfull[x], left_all, TN, preferred_element_type=F32)
        dr = dr.astype(BF16).reshape(jpb, ni, nk)
        for b in range(jpb):
            cb = x * jpb + b
            dsend[cb // 4 * 2 + cb % 2, cb // 2 % 2, 1] = dr[b]
    dl = dl.astype(BF16).reshape(nc, ni, nk)
    for cb in range(nc):
        dsend[cb // 4 * 2 + cb % 2, cb // 2 % 2, 0] = dl[cb]
    spread(npl, m, dc)
    drecv[m] = dsend[m]
    gather(npl, m, dc)

    for half in range(2):
        for side in range(2):
            df[half, side] = drecv[:, half, side].astype(F32)
    for half in range(2):
        for b in range(nq):
            for t in range(t_n):
                i = b * t_n + t
                asend[half * nq + b, t] = jnp.concatenate(
                    [df[half, 0, :, i, :], df[half, 1, :, i, :]], axis=0).astype(BF16)
    spread(nz, z, ac)
    arecv[z] = asend[z]
    gather(nz, z, ac)

    def to_right(b, t):
        return remote(ag.at[b, t], ag.at[b, t], ag_s.at[0, b, t], ag_r.at[b, t],
                      to_ch(lax.rem(q + 1, nq)))

    def to_left(b, t):
        return remote(ag.at[b, t], ag.at[b, t], ag_s.at[1, b, t], ag_r.at[b, t],
                      to_ch(lax.rem(q + nq - 1, nq)))

    def keep(b, t):
        return pltpu.make_async_copy(ag.at[b, t], out.at[b * t_n + t], o_s.at[b, t])

    for t in range(t_n):
        d = jnp.stack([
            jnp.stack([arecv[half * nq + b, t].astype(F32) for half in range(2)])
            for b in range(nq)])
        d0 = d[:, :, :npl].reshape(nq, hq, nk)
        d1 = d[:, :, npl:].reshape(nq, hq, nk)
        f = fo[t]
        gr = jnp.stack([d0 * f[0], d0 * f[1], d1 * f[2], d1 * f[3]], axis=1)
        gr = gr.reshape(nq * 4 * hq, nk).astype(BF16)
        gro[:, t * nk:(t + 1) * nk] = gr
        d_norm = lax.dot_general(gr, wf[...].reshape(nq * 4 * hq, cc),
                                 TN, preferred_element_type=F32)
        e = d_norm * gain_v
        std = stdo[t]
        first = jnp.mean(e, axis=-1, keepdims=True)
        second = jnp.mean(e * std, axis=-1, keepdims=True)
        ag[q, t] = (invo[t] * (e - first - std * second)).astype(BF16)
        keep(q, t).start()

        @pl.when(q < nq - 1)
        def _():
            to_right(q, t).start()

        @pl.when(q > 0)
        def _():
            to_left(q, t).start()

    def relay(s):
        def one(t, carry):
            @pl.when(q >= s)
            def _():
                to_right(q - s, t).wait_recv()

                @pl.when(q < nq - 1)
                def _():
                    to_right(q - s, t).start()
                keep(q - s, t).start()

            @pl.when(q + s < nq)
            def _():
                to_left(q + s, t).wait_recv()

                @pl.when(q > 0)
                def _():
                    to_left(q + s, t).start()
                keep(q + s, t).start()
            return carry
        lax.fori_loop(0, t_n, one, 0)

    def w_own():
        nb = normed[pl.ds(q * t_n, t_n)].reshape(t_n * nk, cc)
        w_part = jnp.dot(gro[...], nb, preferred_element_type=F32).reshape(nq, npl, 8, cc)
        for b in range(npl):
            wp[b] = w_part[:, b]
        spread(npl, m, wa)
        wr[m] = wp[m]

    def w_plane():
        gather(npl, m, wa)
        zp[...] = jnp.sum(wr[...], axis=0)
        spread(nr, r, wx)
        xr[r] = zp[pl.ds(r * qr, qr)]

    def w_rows():
        gather(nr, r, wx)
        total = xr[0]
        for x in range(1, nr):
            total = total + xr[x]
        zq[...] = total
        for half in range(2):
            for a in range(qr):
                to, copy = wz(half, a)

                @pl.when(to != z)
                def _(copy=copy):
                    copy.start()

                @pl.when(to == z)
                def _(a=a):
                    zr[z] = zq[a]

    def w_ring():
        @pl.when(owner)
        def _():
            gather(nz, z, wz_from)
            wg[m] = jnp.sum(zr[...], axis=0) * (1.0 / n)
            spread(nr, r, wb)

    def w_share():
        @pl.when(jnp.logical_not(owner))
        def _():
            wb(r, r).wait_recv()
        spread(npl, m, wd)

    def w_last():
        gather(npl, m, wd)

    steps = {1: [w_own], 2: [w_plane], 3: [w_rows], 5: [w_ring], 6: [w_share]}
    done = set()
    for s in range(1, nq):
        relay(s)
        for step in steps.get(s, ()):
            step()
            done.add(step)
    for at in sorted(steps):
        for step in steps[at]:
            if step not in done:
                step()
    w_last()
    wout[...] = natural(wg[...].reshape(4 * hq, cc))

    spread(nc, c, g1, False)
    spread(nq, q, wfc, False)
    spread(nc, c, lrc, False)
    spread(nr, r, g2, False)
    spread(npl, m, dc, False)
    spread(nz, z, ac, False)
    spread(npl, m, wa, False)
    spread(nr, r, wx, False)
    for half in range(2):
        for a in range(qr):
            to, copy = wz(half, a)

            @pl.when(to != z)
            def _(copy=copy):
                copy.wait_send()

    @pl.when(owner)
    def _():
        spread(nr, r, wb, False)
    spread(npl, m, wd, False)

    def drain(b, carry):
        def one(t, carry):
            @pl.when(jnp.logical_and(b <= q, q < nq - 1))
            def _():
                to_right(b, t).wait_send()

            @pl.when(jnp.logical_and(b >= q, q > 0))
            def _():
                to_left(b, t).wait_send()
            keep(b, t).wait()
            return carry
        return lax.fori_loop(0, t_n, one, carry)
    lax.fori_loop(0, nq, drain, 0)


def body(nr, nc, nq, pair, token_mask, pair_mask, ln_gain, w_in, grad_tri):
    ni, nk, cc = pair.shape
    hq = w_in.shape[2]
    n = nc * ni
    nj = n // nr
    t_n = ni // nq
    npl = nc // 2
    nz = 2 * nq
    wt = jnp.transpose(w_in, (1, 2, 0)).reshape(4 * hq, cc)
    vmem = pl.BlockSpec(memory_space=pltpu.VMEM)
    hbm = pl.BlockSpec(memory_space=pltpu.HBM)
    dma = lambda *s: pltpu.SemaphoreType.DMA(s)
    out, wout = pl.pallas_call(
        functools.partial(kernel, nr, nc, nq),
        out_shape=(
            jax.ShapeDtypeStruct((ni, nk, cc), BF16),
            jax.ShapeDtypeStruct((4 * hq, cc), F32),
        ),
        in_specs=[hbm] * 6,
        out_specs=(hbm, vmem),
        scratch_shapes=[
            pltpu.VMEM((n // nk, nk), jnp.int32),
            pltpu.VMEM((ni, nk, cc), BF16),
            pltpu.VMEM((ni, nk), jnp.int32),
            pltpu.VMEM((1, cc), F32),
            pltpu.VMEM((4 * hq, cc), BF16),
            pltpu.VMEM((ni, nk), F32),
            pltpu.VMEM((4 * hq, cc), BF16),
            pltpu.VMEM((ni, nk, cc), BF16),
            pltpu.VMEM((ni, hq, nk), F32),
            pltpu.VMEM((ni, hq, nk), F32),
            pltpu.VMEM((nc, 2, ni, nk), BF16),
            pltpu.VMEM((nc, 2, ni, nk), BF16),
            pltpu.VMEM((nr, n, nj), BF16),
            pltpu.VMEM((npl, 2, 2, ni, nk), BF16),
            pltpu.VMEM((npl, 2, 2, ni, nk), BF16),
            pltpu.VMEM((2, 2, npl, ni, nk), F32),
            pltpu.VMEM((nz, t_n, hq, nk), BF16),
            pltpu.VMEM((nz, t_n, hq, nk), BF16),
            pltpu.VMEM((nq, 4 * hq, cc), BF16),
            pltpu.VMEM((t_n, 4, nq, hq, nk), F32),
            pltpu.VMEM((t_n, nk, cc), F32),
            pltpu.VMEM((t_n, nk, cc), F32),
            pltpu.VMEM((nq * 4 * hq, t_n * nk), BF16),
            pltpu.VMEM((nq, t_n, nk, cc), BF16),
            pltpu.VMEM((npl, nq, 8, cc), F32),
            pltpu.VMEM((npl, nq, 8, cc), F32),
            pltpu.VMEM((nq, 8, cc), F32),
            pltpu.VMEM((nq // nr, 8, cc), F32),
            pltpu.VMEM((nz, 8, cc), F32),
            pltpu.VMEM((nr, nq // nr, 8, cc), F32),
            pltpu.VMEM((npl, 8, cc), F32),
            dma(5), dma(nq, t_n),
            dma(nc), dma(nc), dma(nr), dma(nr), dma(nq), dma(nq),
            dma(nc), dma(nc), dma(npl), dma(npl), dma(nz), dma(nz),
            dma(2, nq, t_n), dma(nq, t_n),
            dma(npl), dma(npl), dma(nr), dma(nr), dma(2, nq // nr), dma(nz), dma(nr), dma(1),
            dma(npl), dma(npl),
        ],
        compiler_params=pltpu.CompilerParams(
            collective_id=0, has_side_effects=True, vmem_limit_bytes=60 * 1024 * 1024,
        ),
        name="triangle_backward",
    )(token_mask.reshape(n // nk, nk), pair, pair_mask, ln_gain.reshape(1, cc), wt, grad_tri)
    w_grad = jnp.transpose(wout.reshape(4, hq, cc), (2, 0, 1))
    return out, w_grad


def solution(mesh):
    size = dict(mesh.shape)
    return jax.shard_map(
        functools.partial(body, size["row"], size["col"], size["ch"]),
        mesh=mesh,
        in_specs=(
            P("col", "row", None),
            P(),
            P("col", "row"),
            P(),
            P(None, None, "ch"),
            P("ch", "col", None),
        ),
        out_specs=(P("col", "row", None), P(None, None, "ch")),
        check_vma=False,
    )
```

```python
import functools

import jax
import jax.numpy as jnp
from jax import lax
from jax.experimental import pallas as pl
from jax.experimental.pallas import tpu as pltpu
from jax.sharding import PartitionSpec as P

EPS = 1e-05
F32 = jnp.float32
BF16 = jnp.bfloat16
MESH = pl.DeviceIdType.MESH
NT = (((1,), (1,)), ((), ()))
TN = (((0,), (0,)), ((), ()))


def normalise(x):
    mean = jnp.mean(x, axis=-1, keepdims=True)
    cen = x - mean
    inv = lax.rsqrt(jnp.mean(cen * cen, axis=-1, keepdims=True) + EPS)
    return cen * inv, inv


def factors(p, m):
    p0, p1, p2, p3 = p
    s1 = jax.nn.sigmoid(p1)
    s3 = jax.nn.sigmoid(p3)
    f0 = m * s1
    f2 = m * s3
    return f0, f0 * p0 * (1.0 - s1), f2, f2 * p2 * (1.0 - s3)


def kernel(
    nr, nc, nq,
    tok, pair_h, pm_h, gain_h, w_h, gt,
    out, wout,
    tok_v, pair, pm, gain, w_v, gq, mask, wt,
    normed, lt, rt, lrs, lrr, gfull, dsend, drecv, df, asend, arecv,
    wf, wfs, dno, fo, stdo, invo, gro, ag, wp, wr, zp, zq, zr, xr, wg,
    in_s, o_s,
    g1_s, g1_r, g2_s, g2_r, wf_s, wf_r, wx2_s, wx2_r, lr_s, lr_r, d_s, d_r, a_s, a_r,
    ag_s, ag_r, wa_s, wa_r, wx_s, wx_r, wz_s, wz_r, wb_s, wb_r, wd_s, wd_r,
):
    r = lax.axis_index("row")
    c = lax.axis_index("col")
    q = lax.axis_index("ch")
    ni, nk, cc = pair.shape
    hq = nc
    n = nc * ni
    nj = gfull.shape[2]
    t_n = ni // nq
    jpb = nj // ni
    gr_n = 4 // nr
    wr_n = gr_n * hq
    npl = nc // 2
    nz = 2 * nq
    zh = lax.rem(lax.div(c, 2), 2)
    m = lax.div(c, 4) * 2 + lax.rem(c, 2)
    z = zh * nq + q

    def col_of(zh_, m_):
        return (lax.div(m_, 2) * 2 + zh_) * 2 + lax.rem(m_, 2)

    def pos(c_):
        return lax.rem(lax.div(c_, 2), 2) * npl + lax.div(c_, 4) * 2 + lax.rem(c_, 2)

    def to_row(i):
        return {"row": i}

    def to_col(i):
        return {"col": i}

    def to_ch(i):
        return {"ch": i}

    def to_plane(i):
        return {"col": col_of(zh, i)}

    def to_z(i):
        return {"col": col_of(lax.div(i, nq), m), "ch": lax.rem(i, nq)}

    lane = pl.ds(pl.multiple_of(r * nj, nj), nj)
    mine = pltpu.make_async_copy(gt.at[:, :, lane], gq, in_s.at[5])
    mine.start()
    loads = [
        pltpu.make_async_copy(src, dst, in_s.at[k])
        for k, (src, dst) in enumerate(
            ((w_h, w_v), (tok, tok_v), (pm_h, pm), (gain_h, gain), (pair_h, pair)))
    ]
    for load in loads:
        load.start()

    barrier = pltpu.get_barrier_semaphore()

    def greet(device):
        pl.semaphore_signal(barrier, inc=1, device_id=device, device_id_type=MESH)

    def greet_all(size, me, to):
        def one(off, carry):
            greet(to(lax.rem(me + off, size)))
            return carry
        lax.fori_loop(1, size, one, 0)

    greet_all(nr, r, to_row)
    greet_all(nc, c, to_col)
    greet_all(nq, q, to_ch)

    def greet_far(off, carry):
        greet({"col": col_of(1 - zh, m), "ch": lax.rem(q + off, nq)})
        return carry
    lax.fori_loop(1, nq, greet_far, 0)

    def permuted(w):
        rows = []
        for g in range(4):
            for half in range(2):
                for y in range(nc // 4):
                    at = g * hq + (y * 2 + half) * 2
                    rows.append(w[at:at + 2])
        return jnp.concatenate(rows, axis=0)

    def natural(w):
        rows = []
        for g in range(4):
            for y in range(nc // 4):
                for half in range(2):
                    at = g * hq + half * npl + y * 2
                    rows.append(w[at:at + 2])
        return jnp.concatenate(rows, axis=0)

    def remote(src, dst, s, rr, device):
        return pltpu.make_async_remote_copy(
            src_ref=src, dst_ref=dst, send_sem=s, recv_sem=rr,
            device_id=device, device_id_type=MESH,
        )

    def spread(size, me, make, start=True):
        def one(off, carry):
            to = lax.rem(me + off, size)
            copy = make(to, me)
            if start:
                copy.start()
            else:
                copy.wait_send()
            return carry
        lax.fori_loop(1, size, one, 0)

    def gather(size, me, make):
        def one(off, carry):
            src = lax.rem(me + off, size)
            make(src, src).wait_recv()
            return carry
        lax.fori_loop(1, size, one, 0)


    def rows_of(b):
        return pl.ds(pl.multiple_of(b * ni, ni), ni)

    def g1(to, src):
        return remote(gq.at[to], gfull.at[r, rows_of(src)],
                      g1_s.at[to], g1_r.at[src], to_col(to))

    def g2(to, src):
        return remote(gfull.at[src], gfull.at[src], g2_s.at[to], g2_r.at[src], to_row(to))

    def wfc(to, src):
        part = wt.at[pl.ds(pl.multiple_of(r * wr_n, wr_n), wr_n)]
        return remote(part, wf.at[r, src], wf_s.at[to], wf_r.at[src], to_ch(to))

    def wfx(to, src):
        return remote(wf.at[src], wf.at[src], wx2_s.at[to], wx2_r.at[src], to_row(to))

    def lrc(side):
        def make(to, src):
            return remote(lrs.at[side, pos(to)], lrr.at[side, src],
                          lr_s.at[side, to], lr_r.at[side, src], to_col(to))
        return make

    def dc(side):
        def make(to, src):
            return remote(dsend.at[side, to], drecv.at[side, src],
                          d_s.at[side, to], d_r.at[side, src], to_plane(to))
        return make

    def ac(side, u):
        def make(to, src):
            return remote(asend.at[side, u, to], arecv.at[side, u, src],
                          a_s.at[side, u, to], a_r.at[side, u, src], to_z(to))
        return make

    def wa(to, src):
        return remote(wp.at[to], wr.at[src], wa_s.at[to], wa_r.at[src], to_plane(to))

    qr = nq // nr
    owner = lax.div(q, qr) == r

    def wx(to, src):
        return remote(zp.at[pl.ds(to * qr, qr)], xr.at[src], wx_s.at[to], wx_r.at[src],
                      to_row(to))

    def wz(half, a):
        to = half * nq + r * qr + a
        return to, remote(zq.at[a], zr.at[z], wz_s.at[half, a], wz_r.at[z], to_z(to))

    def wz_from(to, src):
        return remote(zq.at[0], zr.at[src], wz_s.at[0, 0], wz_r.at[src], to_z(to))

    def wb(to, src):
        return remote(wg.at[m], wg.at[m], wb_s.at[to], wb_r.at[0], to_row(to))

    def wd(to, src):
        return remote(wg.at[src], wg.at[src], wd_s.at[to], wd_r.at[src], to_plane(to))

    pl.semaphore_wait(barrier, nr + nc + 2 * nq - 4)
    mine.wait()
    spread(nc, c, g1)
    for load in loads:
        load.wait()
    wv = permuted(w_v[...].astype(F32)).astype(BF16)
    wt[...] = wv
    wf[r, q] = wt[pl.ds(pl.multiple_of(r * wr_n, wr_n), wr_n), :]

    tok_k = tok_v[pl.ds(r, 1), :]
    first = c * ni
    tok_i = tok_v[pl.ds(lax.div(first, nk), 1), :]
    at = lax.broadcasted_iota(jnp.int32, (ni, nk), 1) - lax.rem(first, nk)
    hit = at == lax.broadcasted_iota(jnp.int32, (ni, nk), 0)
    tok_i = jnp.sum(jnp.where(hit, tok_i, 0).astype(F32), axis=1, keepdims=True)
    mask[...] = (pm[...] * tok_k).astype(F32) * tok_i
    gain_v = gain[...]

    spread(nq, q, wfc)
    gfull[r, rows_of(c)] = gq[c]

    def mask_of(i):
        return mask[pl.ds(i, 1), :]

    def project(i, carry):
        std, _ = normalise(pair[i].astype(F32))
        nb = (std * gain_v).astype(BF16)
        normed[i] = nb
        p = lax.dot_general(wt[...], nb, NT, preferred_element_type=F32)
        p = p.reshape(4, hq, nk)
        mk = mask_of(i)
        lt[i] = mk * jax.nn.sigmoid(p[1]) * p[0]
        rt[i] = mk * jax.nn.sigmoid(p[3]) * p[2]
        return carry

    lax.fori_loop(0, ni, project, 0, unroll=4)

    for side, made in ((0, lt), (1, rt)):
        for h in range(hq):
            lrs[side, h] = made[:, h, :].astype(BF16)
        spread(nc, c, lrc(side))
        lrr[side, c] = lrs[side, pos(c)]

    gather(nc, c, g1)
    spread(nr, r, g2)

    gather(nq, q, wfc)
    spread(nr, r, wfx)
    gather(nr, r, wfx)

    def own(t, carry):
        i = q * t_n + t
        std, inv = normalise(pair[i].astype(F32))
        stdo[t] = std
        invo[t] = jnp.broadcast_to(inv, (nk, cc))
        p = lax.dot_general(wf[...].reshape(nq * 4 * hq, cc), normed[i], NT,
                            preferred_element_type=F32)
        p = p.reshape(nr, nq, gr_n, hq, nk)
        f = factors(tuple(p[g // gr_n, :, g % gr_n] for g in range(4)), mask_of(i))
        for g in range(4):
            fo[t, g] = f[g]
        return carry

    tu = t_n // 2

    def return_side(side, d):
        for cb in range(nc):
            dsend[side, cb // 4 * 2 + cb % 2, cb // 2 % 2] = d[cb]
        spread(npl, m, dc(side))
        drecv[side, m] = dsend[side, m]

    def forward_side(side):
        gather(npl, m, dc(side))
        for half in range(2):
            df[half] = drecv[side, :, half].astype(F32)
        for u in range(tu):
            for half in range(2):
                for b in range(nq):
                    i = b * t_n + 2 * u
                    asend[side, u, half * nq + b] = jnp.concatenate(
                        [df[half, :, i, :], df[half, :, i + 1, :]], axis=0).astype(BF16)
            spread(nz, z, ac(side, u))
            arecv[side, u, z] = asend[side, u, z]

    lax.fori_loop(0, tu, own, 0)
    gather(nr, r, g2)
    gather(nc, c, lrc(0))
    left_all = lrr[0].reshape(n, nk)
    dr = []
    for x in range(nr):
        d = lax.dot_general(gfull[x], left_all, TN, preferred_element_type=F32)
        dr.append(d.astype(BF16).reshape(jpb, ni, nk))
    return_side(1, [dr[cb // jpb][cb % jpb] for cb in range(nc)])
    lax.fori_loop(tu, t_n, own, 0)
    for side in range(2):
        for b in range(nq):
            for gg in range(2):
                g, row = side * 2 + gg, (b * 2 + gg) * hq
                at = g % gr_n * hq
                wfs[side, row:row + hq] = wf[g // gr_n, b, at:at + hq]
    forward_side(1)

    gather(nc, c, lrc(1))
    dl = jnp.zeros((n, nk), F32)
    for x in range(nr):
        rx = lrr[1, x * jpb:(x + 1) * jpb].reshape(nj, nk)
        dl = dl + jnp.dot(gfull[x], rx, preferred_element_type=F32)
    dl = dl.astype(BF16).reshape(nc, ni, nk)
    return_side(0, [dl[cb] for cb in range(nc)])
    forward_side(0)

    def side_grads(side, t):
        u, at = t // 2, t % 2 * npl
        d = jnp.stack([
            jnp.stack([arecv[side, u, half * nq + b].astype(F32)[at:at + npl]
                       for half in range(2)])
            for b in range(nq)]).reshape(nq, hq, nk)
        gr = jnp.stack([d * fo[t, 2 * side], d * fo[t, 2 * side + 1]], axis=1)
        gr = gr.reshape(nq * 2 * hq, nk).astype(BF16)
        gro[side, :, t * nk:(t + 1) * nk] = gr
        return lax.dot_general(gr, wfs[side], TN, preferred_element_type=F32)

    def w_side(side):
        nb = normed[pl.ds(q * t_n, t_n)].reshape(t_n * nk, cc)
        part = jnp.dot(gro[side], nb, preferred_element_type=F32)
        part = part.reshape(nq, npl // 2, 8, cc)
        for b in range(npl // 2):
            wp[side * (npl // 2) + b] = part[:, b]

    for u in range(tu):
        gather(nz, z, ac(1, u))
    for t in range(t_n):
        dno[t] = side_grads(1, t)
    w_side(1)

    def to_right(b, t):
        return remote(ag.at[b, t], ag.at[b, t], ag_s.at[0, b, t], ag_r.at[b, t],
                      to_ch(lax.rem(q + 1, nq)))

    def to_left(b, t):
        return remote(ag.at[b, t], ag.at[b, t], ag_s.at[1, b, t], ag_r.at[b, t],
                      to_ch(lax.rem(q + nq - 1, nq)))

    def keep(b, t):
        return pltpu.make_async_copy(ag.at[b, t], out.at[b * t_n + t], o_s.at[b, t])

    def relay_one(s, t):
        @pl.when(q >= s)
        def _():
            to_right(q - s, t).wait_recv()

            @pl.when(q < nq - 1)
            def _():
                to_right(q - s, t).start()
            keep(q - s, t).start()

        @pl.when(q + s < nq)
        def _():
            to_left(q + s, t).wait_recv()

            @pl.when(q > 0)
            def _():
                to_left(q + s, t).start()
            keep(q + s, t).start()

    def relay(s):
        def one(t, carry):
            relay_one(s, t)
            return carry
        lax.fori_loop(0, t_n, one, 0)

    for t in range(t_n):
        if t % 2 == 0:
            gather(nz, z, ac(0, t // 2))
        e = (side_grads(0, t) + dno[t]) * gain_v
        std = stdo[t]
        first = jnp.mean(e, axis=-1, keepdims=True)
        second = jnp.mean(e * std, axis=-1, keepdims=True)
        ag[q, t] = (invo[t] * (e - first - std * second)).astype(BF16)
        keep(q, t).start()

        @pl.when(q < nq - 1)
        def _():
            to_right(q, t).start()

        @pl.when(q > 0)
        def _():
            to_left(q, t).start()

    def w_own():
        w_side(0)
        spread(npl, m, wa)
        wr[m] = wp[m]

    def w_plane():
        gather(npl, m, wa)
        zp[...] = jnp.sum(wr[...], axis=0)
        spread(nr, r, wx)
        xr[r] = zp[pl.ds(r * qr, qr)]

    def w_rows():
        gather(nr, r, wx)
        total = xr[0]
        for x in range(1, nr):
            total = total + xr[x]
        zq[...] = total
        for half in range(2):
            for a in range(qr):
                to, copy = wz(half, a)

                @pl.when(to != z)
                def _(copy=copy):
                    copy.start()

                @pl.when(to == z)
                def _(a=a):
                    zr[z] = zq[a]

    def w_ring():
        @pl.when(owner)
        def _():
            gather(nz, z, wz_from)
            wg[m] = jnp.sum(zr[...], axis=0) * (1.0 / n)
            spread(nr, r, wb)

    def w_share():
        @pl.when(jnp.logical_not(owner))
        def _():
            wb(r, r).wait_recv()
        spread(npl, m, wd)

    def w_last():
        gather(npl, m, wd)

    steps = {1: [w_own], 2: [w_plane], 3: [w_rows], 5: [w_ring], 6: [w_share]}
    done = set()
    for s in range(1, nq):
        relay(s)
        for step in steps.get(s, ()):
            step()
            done.add(step)
    for at in sorted(steps):
        for step in steps[at]:
            if step not in done:
                step()
    w_last()
    wout[...] = natural(wg[...].reshape(4 * hq, cc))

    spread(nc, c, g1, False)
    spread(nq, q, wfc, False)
    spread(nr, r, wfx, False)
    for side in range(2):
        spread(nc, c, lrc(side), False)
    spread(nr, r, g2, False)
    for side in range(2):
        spread(npl, m, dc(side), False)
        for u in range(tu):
            spread(nz, z, ac(side, u), False)
    spread(npl, m, wa, False)
    spread(nr, r, wx, False)
    for half in range(2):
        for a in range(qr):
            to, copy = wz(half, a)

            @pl.when(to != z)
            def _(copy=copy):
                copy.wait_send()

    @pl.when(owner)
    def _():
        spread(nr, r, wb, False)
    spread(npl, m, wd, False)

    def drain(b, carry):
        def one(t, carry):
            @pl.when(jnp.logical_and(b <= q, q < nq - 1))
            def _():
                to_right(b, t).wait_send()

            @pl.when(jnp.logical_and(b >= q, q > 0))
            def _():
                to_left(b, t).wait_send()
            keep(b, t).wait()
            return carry
        return lax.fori_loop(0, t_n, one, carry)
    lax.fori_loop(0, nq, drain, 0)


def body(nr, nc, nq, pair, token_mask, pair_mask, ln_gain, w_in, grad_tri):
    ni, nk, cc = pair.shape
    hq = w_in.shape[2]
    n = nc * ni
    nj = n // nr
    t_n = ni // nq
    npl = nc // 2
    nz = 2 * nq
    wt = jnp.transpose(w_in, (1, 2, 0)).reshape(4 * hq, cc)
    vmem = pl.BlockSpec(memory_space=pltpu.VMEM)
    hbm = pl.BlockSpec(memory_space=pltpu.HBM)
    dma = lambda *s: pltpu.SemaphoreType.DMA(s)
    out, wout = pl.pallas_call(
        functools.partial(kernel, nr, nc, nq),
        out_shape=(
            jax.ShapeDtypeStruct((ni, nk, cc), BF16),
            jax.ShapeDtypeStruct((4 * hq, cc), F32),
        ),
        in_specs=[hbm] * 6,
        out_specs=(hbm, vmem),
        scratch_shapes=[
            pltpu.VMEM((n // nk, nk), jnp.int32),
            pltpu.VMEM((ni, nk, cc), BF16),
            pltpu.VMEM((ni, nk), jnp.int32),
            pltpu.VMEM((1, cc), F32),
            pltpu.VMEM((4 * hq, cc), BF16),
            pltpu.VMEM((nc, ni, nj), BF16),
            pltpu.VMEM((ni, nk), F32),
            pltpu.VMEM((4 * hq, cc), BF16),
            pltpu.VMEM((ni, nk, cc), BF16),
            pltpu.VMEM((ni, hq, nk), F32),
            pltpu.VMEM((ni, hq, nk), F32),
            pltpu.VMEM((2, nc, ni, nk), BF16),
            pltpu.VMEM((2, nc, ni, nk), BF16),
            pltpu.VMEM((nr, n, nj), BF16),
            pltpu.VMEM((2, npl, 2, ni, nk), BF16),
            pltpu.VMEM((2, npl, 2, ni, nk), BF16),
            pltpu.VMEM((2, npl, ni, nk), F32),
            pltpu.VMEM((2, t_n // 2, nz, hq, nk), BF16),
            pltpu.VMEM((2, t_n // 2, nz, hq, nk), BF16),
            pltpu.VMEM((nr, nq, 4 // nr * hq, cc), BF16),
            pltpu.VMEM((2, nq * 2 * hq, cc), BF16),
            pltpu.VMEM((t_n, nk, cc), F32),
            pltpu.VMEM((t_n, 4, nq, hq, nk), F32),
            pltpu.VMEM((t_n, nk, cc), F32),
            pltpu.VMEM((t_n, nk, cc), F32),
            pltpu.VMEM((2, nq * 2 * hq, t_n * nk), BF16),
            pltpu.VMEM((nq, t_n, nk, cc), BF16),
            pltpu.VMEM((npl, nq, 8, cc), F32),
            pltpu.VMEM((npl, nq, 8, cc), F32),
            pltpu.VMEM((nq, 8, cc), F32),
            pltpu.VMEM((nq // nr, 8, cc), F32),
            pltpu.VMEM((nz, 8, cc), F32),
            pltpu.VMEM((nr, nq // nr, 8, cc), F32),
            pltpu.VMEM((npl, 8, cc), F32),
            dma(6), dma(nq, t_n),
            dma(nc), dma(nc), dma(nr), dma(nr), dma(nq), dma(nq), dma(nr), dma(nr),
            dma(2, nc), dma(2, nc), dma(2, npl), dma(2, npl),
            dma(2, t_n // 2, nz), dma(2, t_n // 2, nz),
            dma(2, nq, t_n), dma(nq, t_n),
            dma(npl), dma(npl), dma(nr), dma(nr), dma(2, nq // nr), dma(nz), dma(nr), dma(1),
            dma(npl), dma(npl),
        ],
        compiler_params=pltpu.CompilerParams(
            collective_id=0, has_side_effects=True, vmem_limit_bytes=60 * 1024 * 1024,
        ),
        name="triangle_backward",
    )(token_mask.reshape(n // nk, nk), pair, pair_mask, ln_gain.reshape(1, cc), wt, grad_tri)
    w_grad = jnp.transpose(wout.reshape(4, hq, cc), (2, 0, 1))
    return out, w_grad


def solution(mesh):
    size = dict(mesh.shape)
    return jax.shard_map(
        functools.partial(body, size["row"], size["col"], size["ch"]),
        mesh=mesh,
        in_specs=(
            P("col", "row", None),
            P(),
            P("col", "row"),
            P(),
            P(None, None, "ch"),
            P("ch", "col", None),
        ),
        out_specs=(P("col", "row", None), P(None, None, "ch")),
        check_vma=False,
    )
```

```python
import functools

import jax
import jax.numpy as jnp
from jax import lax
from jax.experimental import pallas as pl
from jax.experimental.pallas import tpu as pltpu
from jax.sharding import PartitionSpec as P

EPS = 1e-05
F32 = jnp.float32
BF16 = jnp.bfloat16
MESH = pl.DeviceIdType.MESH
NT = (((1,), (1,)), ((), ()))
TN = (((0,), (0,)), ((), ()))


def normalise(x):
    mean = jnp.mean(x, axis=-1, keepdims=True)
    cen = x - mean
    inv = lax.rsqrt(jnp.mean(cen * cen, axis=-1, keepdims=True) + EPS)
    return cen * inv, inv


def factors(p, m):
    p0, p1, p2, p3 = p
    s1 = jax.nn.sigmoid(p1)
    s3 = jax.nn.sigmoid(p3)
    f0 = m * s1
    f2 = m * s3
    return f0, f0 * p0 * (1.0 - s1), f2, f2 * p2 * (1.0 - s3)


def kernel(
    nr, nc, nq,
    tok, pair_h, pm_h, gain_h, w_h, gt,
    out, wout,
    tok_v, pair, pm, gain, w_v, gq, mask, wt,
    normed, lt, rt, lrs, lrr, gfull, dsend, drecv, df, asend, arecv,
    wf, wfs, dno, fo, stdo, invo, gro, ag, wp, wr, zp, zq, zr, xr, wg,
    in_s, o_s,
    g1_s, g1_r, g2_s, g2_r, wf_s, wf_r, wx2_s, wx2_r, lr_s, lr_r, d_s, d_r, a_s, a_r,
    ag_s, ag_r, wa_s, wa_r, wx_s, wx_r, wz_s, wz_r, wb_s, wb_r, wd_s, wd_r,
):
    r = lax.axis_index("row")
    c = lax.axis_index("col")
    q = lax.axis_index("ch")
    ni, nk, cc = pair.shape
    hq = nc
    n = nc * ni
    nj = gfull.shape[2]
    t_n = ni // nq
    jpb = nj // ni
    gr_n = 4 // nr
    wr_n = gr_n * hq
    npl = nc // 2
    nz = 2 * nq
    zh = lax.rem(lax.div(c, 2), 2)
    m = lax.div(c, 4) * 2 + lax.rem(c, 2)
    z = zh * nq + q

    def col_of(zh_, m_):
        return (lax.div(m_, 2) * 2 + zh_) * 2 + lax.rem(m_, 2)

    def pos(c_):
        return lax.rem(lax.div(c_, 2), 2) * npl + lax.div(c_, 4) * 2 + lax.rem(c_, 2)

    def to_row(i):
        return {"row": i}

    def to_col(i):
        return {"col": i}

    def to_ch(i):
        return {"ch": i}

    def to_plane(i):
        return {"col": col_of(zh, i)}

    def to_z(i):
        return {"col": col_of(lax.div(i, nq), m), "ch": lax.rem(i, nq)}

    lane = pl.ds(pl.multiple_of(r * nj, nj), nj)
    mine = pltpu.make_async_copy(gt.at[:, :, lane], gq, in_s.at[5])
    mine.start()
    loads = [
        pltpu.make_async_copy(src, dst, in_s.at[k])
        for k, (src, dst) in enumerate(
            ((w_h, w_v), (tok, tok_v), (pm_h, pm), (gain_h, gain), (pair_h, pair)))
    ]
    for load in loads:
        load.start()

    barrier = pltpu.get_barrier_semaphore()

    def greet(device):
        pl.semaphore_signal(barrier, inc=1, device_id=device, device_id_type=MESH)

    def greet_all(size, me, to):
        def one(off, carry):
            greet(to(lax.rem(me + off, size)))
            return carry
        lax.fori_loop(1, size, one, 0)

    greet_all(nr, r, to_row)
    greet_all(nc, c, to_col)
    greet_all(nq, q, to_ch)

    def greet_far(off, carry):
        greet({"col": col_of(1 - zh, m), "ch": lax.rem(q + off, nq)})
        return carry
    lax.fori_loop(1, nq, greet_far, 0)

    def permuted(w):
        rows = []
        for g in range(4):
            for half in range(2):
                for y in range(nc // 4):
                    at = g * hq + (y * 2 + half) * 2
                    rows.append(w[at:at + 2])
        return jnp.concatenate(rows, axis=0)

    def natural(w):
        rows = []
        for g in range(4):
            for y in range(nc // 4):
                for half in range(2):
                    at = g * hq + half * npl + y * 2
                    rows.append(w[at:at + 2])
        return jnp.concatenate(rows, axis=0)

    def remote(src, dst, s, rr, device):
        return pltpu.make_async_remote_copy(
            src_ref=src, dst_ref=dst, send_sem=s, recv_sem=rr,
            device_id=device, device_id_type=MESH,
        )

    def spread(size, me, make, start=True):
        def one(off, carry):
            to = lax.rem(me + off, size)
            copy = make(to, me)
            if start:
                copy.start()
            else:
                copy.wait_send()
            return carry
        lax.fori_loop(1, size, one, 0)

    def gather(size, me, make):
        def one(off, carry):
            src = lax.rem(me + off, size)
            make(src, src).wait_recv()
            return carry
        lax.fori_loop(1, size, one, 0)


    def rows_of(b):
        return pl.ds(pl.multiple_of(b * ni, ni), ni)

    def g1(to, src):
        return remote(gq.at[to], gfull.at[r, rows_of(src)],
                      g1_s.at[to], g1_r.at[src], to_col(to))

    def g2(to, src):
        return remote(gfull.at[src], gfull.at[src], g2_s.at[to], g2_r.at[src], to_row(to))

    def wfc(to, src):
        part = wt.at[pl.ds(pl.multiple_of(r * wr_n, wr_n), wr_n)]
        return remote(part, wf.at[r, src], wf_s.at[to], wf_r.at[src], to_ch(to))

    def wfx(to, src):
        return remote(wf.at[src], wf.at[src], wx2_s.at[to], wx2_r.at[src], to_row(to))

    def lrc(side):
        def make(to, src):
            return remote(lrs.at[side, pos(to)], lrr.at[side, src],
                          lr_s.at[side, to], lr_r.at[side, src], to_col(to))
        return make

    def dc(side):
        def make(to, src):
            return remote(dsend.at[side, to], drecv.at[side, src],
                          d_s.at[side, to], d_r.at[side, src], to_plane(to))
        return make

    def ac(side, u):
        def make(to, src):
            return remote(asend.at[side, u, to], arecv.at[side, u, src],
                          a_s.at[side, u, to], a_r.at[side, u, src], to_z(to))
        return make

    def wa(to, src):
        return remote(wp.at[to], wr.at[src], wa_s.at[to], wa_r.at[src], to_plane(to))

    qr = nq // nr
    owner = lax.div(q, qr) == r

    def wx(to, src):
        return remote(zp.at[pl.ds(to * qr, qr)], xr.at[src], wx_s.at[to], wx_r.at[src],
                      to_row(to))

    def wz(half, a):
        to = half * nq + r * qr + a
        return to, remote(zq.at[a], zr.at[z], wz_s.at[half, a], wz_r.at[z], to_z(to))

    def wz_from(to, src):
        return remote(zq.at[0], zr.at[src], wz_s.at[0, 0], wz_r.at[src], to_z(to))

    def wb(to, src):
        return remote(wg.at[m], wg.at[m], wb_s.at[to], wb_r.at[0], to_row(to))

    def wd(to, src):
        return remote(wg.at[src], wg.at[src], wd_s.at[to], wd_r.at[src], to_plane(to))

    pl.semaphore_wait(barrier, nr + nc + 2 * nq - 4)
    mine.wait()
    spread(nc, c, g1)
    for load in loads:
        load.wait()
    wv = permuted(w_v[...].astype(F32)).astype(BF16)
    wt[...] = wv
    wf[r, q] = wt[pl.ds(pl.multiple_of(r * wr_n, wr_n), wr_n), :]

    tok_k = tok_v[pl.ds(r, 1), :]
    first = c * ni
    tok_i = tok_v[pl.ds(lax.div(first, nk), 1), :]
    at = lax.broadcasted_iota(jnp.int32, (ni, nk), 1) - lax.rem(first, nk)
    hit = at == lax.broadcasted_iota(jnp.int32, (ni, nk), 0)
    tok_i = jnp.sum(jnp.where(hit, tok_i, 0).astype(F32), axis=1, keepdims=True)
    mask[...] = (pm[...] * tok_k).astype(F32) * tok_i
    gain_v = gain[...]

    spread(nq, q, wfc)
    gfull[r, rows_of(c)] = gq[c]

    def mask_of(i):
        return mask[pl.ds(i, 1), :]

    def project(i, carry):
        std, _ = normalise(pair[i].astype(F32))
        nb = (std * gain_v).astype(BF16)
        normed[i] = nb
        p = lax.dot_general(wt[...], nb, NT, preferred_element_type=F32)
        p = p.reshape(4, hq, nk)
        mk = mask_of(i)
        lt[i] = mk * jax.nn.sigmoid(p[1]) * p[0]
        rt[i] = mk * jax.nn.sigmoid(p[3]) * p[2]
        return carry

    lax.fori_loop(0, ni, project, 0, unroll=4)

    for side, made in ((0, lt), (1, rt)):
        for h in range(hq):
            lrs[side, h] = made[:, h, :].astype(BF16)
        spread(nc, c, lrc(side))
        lrr[side, c] = lrs[side, pos(c)]

    gather(nc, c, g1)
    spread(nr, r, g2)

    gather(nq, q, wfc)
    spread(nr, r, wfx)
    gather(nr, r, wfx)

    def own(t, carry):
        i = q * t_n + t
        std, inv = normalise(pair[i].astype(F32))
        stdo[t] = std
        invo[t] = jnp.broadcast_to(inv, (nk, cc))
        p = lax.dot_general(wf[...].reshape(nq * 4 * hq, cc), normed[i], NT,
                            preferred_element_type=F32)
        p = p.reshape(nr, nq, gr_n, hq, nk)
        f = factors(tuple(p[g // gr_n, :, g % gr_n] for g in range(4)), mask_of(i))
        for g in range(4):
            fo[t, g] = f[g]
        return carry

    tu = t_n // 2

    def return_side(side, d):
        for cb in range(nc):
            dsend[side, cb // 4 * 2 + cb % 2, cb // 2 % 2] = d[cb]
        spread(npl, m, dc(side))
        drecv[side, m] = dsend[side, m]

    def forward_side(side):
        gather(npl, m, dc(side))
        for half in range(2):
            df[half] = drecv[side, :, half].astype(F32)
        for u in range(tu):
            for half in range(2):
                for b in range(nq):
                    i = b * t_n + 2 * u
                    asend[side, u, half * nq + b] = jnp.concatenate(
                        [df[half, :, i, :], df[half, :, i + 1, :]], axis=0).astype(BF16)
            spread(nz, z, ac(side, u))
            arecv[side, u, z] = asend[side, u, z]

    lax.fori_loop(0, tu, own, 0)
    gather(nr, r, g2)
    gather(nc, c, lrc(0))
    left_all = lrr[0].reshape(n, nk)
    dr = []
    for x in range(nr):
        d = lax.dot_general(gfull[x], left_all, TN, preferred_element_type=F32)
        dr.append(d.astype(BF16).reshape(jpb, ni, nk))
    return_side(1, [dr[cb // jpb][cb % jpb] for cb in range(nc)])
    lax.fori_loop(tu, t_n, own, 0)
    for side in range(2):
        for b in range(nq):
            for gg in range(2):
                g, row = side * 2 + gg, (b * 2 + gg) * hq
                at = g % gr_n * hq
                wfs[side, row:row + hq] = wf[g // gr_n, b, at:at + hq]
    forward_side(1)

    gather(nc, c, lrc(1))
    dl = jnp.zeros((n, nk), F32)
    for x in range(nr):
        rx = lrr[1, x * jpb:(x + 1) * jpb].reshape(nj, nk)
        dl = dl + jnp.dot(gfull[x], rx, preferred_element_type=F32)
    dl = dl.astype(BF16).reshape(nc, ni, nk)
    return_side(0, [dl[cb] for cb in range(nc)])
    forward_side(0)

    def side_grads(side, t):
        u, at = t // 2, t % 2 * npl
        d = jnp.stack([
            jnp.stack([arecv[side, u, half * nq + b].astype(F32)[at:at + npl]
                       for half in range(2)])
            for b in range(nq)]).reshape(nq, hq, nk)
        gr = jnp.stack([d * fo[t, 2 * side], d * fo[t, 2 * side + 1]], axis=1)
        gr = gr.reshape(nq * 2 * hq, nk).astype(BF16)
        gro[side, :, t * nk:(t + 1) * nk] = gr
        return lax.dot_general(gr, wfs[side], TN, preferred_element_type=F32)

    def w_side(side):
        nb = normed[pl.ds(q * t_n, t_n)].reshape(t_n * nk, cc)
        part = jnp.dot(gro[side], nb, preferred_element_type=F32)
        part = part.reshape(nq, npl // 2, 8, cc)
        for b in range(npl // 2):
            wp[side * (npl // 2) + b] = part[:, b]

    for u in range(tu):
        gather(nz, z, ac(1, u))
    for t in range(t_n):
        dno[t] = side_grads(1, t)
    w_side(1)

    def to_right(b, t):
        return remote(ag.at[b, t], ag.at[b, t], ag_s.at[0, b, t], ag_r.at[b, t],
                      to_ch(lax.rem(q + 1, nq)))

    def to_left(b, t):
        return remote(ag.at[b, t], ag.at[b, t], ag_s.at[1, b, t], ag_r.at[b, t],
                      to_ch(lax.rem(q + nq - 1, nq)))

    def keep(b, t):
        return pltpu.make_async_copy(ag.at[b, t], out.at[b * t_n + t], o_s.at[b, t])

    def relay_one(s, t):
        @pl.when(q >= s)
        def _():
            to_right(q - s, t).wait_recv()

            @pl.when(q < nq - 1)
            def _():
                to_right(q - s, t).start()
            keep(q - s, t).start()

        @pl.when(q + s < nq)
        def _():
            to_left(q + s, t).wait_recv()

            @pl.when(q > 0)
            def _():
                to_left(q + s, t).start()
            keep(q + s, t).start()

    def relay(s):
        def one(t, carry):
            relay_one(s, t)
            return carry
        lax.fori_loop(0, t_n, one, 0)

    for t in range(t_n):
        if t % 2 == 0:
            gather(nz, z, ac(0, t // 2))
        e = (side_grads(0, t) + dno[t]) * gain_v
        std = stdo[t]
        first = jnp.mean(e, axis=-1, keepdims=True)
        second = jnp.mean(e * std, axis=-1, keepdims=True)
        ag[q, t] = (invo[t] * (e - first - std * second)).astype(BF16)
        keep(q, t).start()

        @pl.when(q < nq - 1)
        def _():
            to_right(q, t).start()

        @pl.when(q > 0)
        def _():
            to_left(q, t).start()

    def w_own():
        w_side(0)
        spread(npl, m, wa)
        wr[m] = wp[m]

    def w_plane():
        gather(npl, m, wa)
        zp[...] = jnp.sum(wr[...], axis=0)
        spread(nr, r, wx)
        xr[r] = zp[pl.ds(r * qr, qr)]

    def w_rows():
        gather(nr, r, wx)
        total = xr[0]
        for x in range(1, nr):
            total = total + xr[x]
        zq[...] = total
        for half in range(2):
            for a in range(qr):
                to, copy = wz(half, a)

                @pl.when(to != z)
                def _(copy=copy):
                    copy.start()

                @pl.when(to == z)
                def _(a=a):
                    zr[z] = zq[a]

    def w_ring():
        @pl.when(owner)
        def _():
            gather(nz, z, wz_from)
            wg[m] = jnp.sum(zr[...], axis=0) * (1.0 / n)
            spread(nr, r, wb)

    def w_share():
        @pl.when(jnp.logical_not(owner))
        def _():
            wb(r, r).wait_recv()
        spread(npl, m, wd)

    def w_last():
        gather(npl, m, wd)

    steps = {0: [w_own], 1: [w_plane], 2: [w_rows], 4: [w_ring], 5: [w_share]}
    done = set()
    for s in range(nq):
        if s > 0:
            relay(s)
        for step in steps.get(s, ()):
            step()
            done.add(step)
    for at in sorted(steps):
        for step in steps[at]:
            if step not in done:
                step()
    w_last()
    wout[...] = natural(wg[...].reshape(4 * hq, cc))

    spread(nc, c, g1, False)
    spread(nq, q, wfc, False)
    spread(nr, r, wfx, False)
    for side in range(2):
        spread(nc, c, lrc(side), False)
    spread(nr, r, g2, False)
    for side in range(2):
        spread(npl, m, dc(side), False)
        for u in range(tu):
            spread(nz, z, ac(side, u), False)
    spread(npl, m, wa, False)
    spread(nr, r, wx, False)
    for half in range(2):
        for a in range(qr):
            to, copy = wz(half, a)

            @pl.when(to != z)
            def _(copy=copy):
                copy.wait_send()

    @pl.when(owner)
    def _():
        spread(nr, r, wb, False)
    spread(npl, m, wd, False)

    def drain(b, carry):
        def one(t, carry):
            @pl.when(jnp.logical_and(b <= q, q < nq - 1))
            def _():
                to_right(b, t).wait_send()

            @pl.when(jnp.logical_and(b >= q, q > 0))
            def _():
                to_left(b, t).wait_send()
            keep(b, t).wait()
            return carry
        return lax.fori_loop(0, t_n, one, carry)
    lax.fori_loop(0, nq, drain, 0)


def body(nr, nc, nq, pair, token_mask, pair_mask, ln_gain, w_in, grad_tri):
    ni, nk, cc = pair.shape
    hq = w_in.shape[2]
    n = nc * ni
    nj = n // nr
    t_n = ni // nq
    npl = nc // 2
    nz = 2 * nq
    wt = jnp.transpose(w_in, (1, 2, 0)).reshape(4 * hq, cc)
    vmem = pl.BlockSpec(memory_space=pltpu.VMEM)
    hbm = pl.BlockSpec(memory_space=pltpu.HBM)
    dma = lambda *s: pltpu.SemaphoreType.DMA(s)
    out, wout = pl.pallas_call(
        functools.partial(kernel, nr, nc, nq),
        out_shape=(
            jax.ShapeDtypeStruct((ni, nk, cc), BF16),
            jax.ShapeDtypeStruct((4 * hq, cc), F32),
        ),
        in_specs=[hbm] * 6,
        out_specs=(hbm, vmem),
        scratch_shapes=[
            pltpu.VMEM((n // nk, nk), jnp.int32),
            pltpu.VMEM((ni, nk, cc), BF16),
            pltpu.VMEM((ni, nk), jnp.int32),
            pltpu.VMEM((1, cc), F32),
            pltpu.VMEM((4 * hq, cc), BF16),
            pltpu.VMEM((nc, ni, nj), BF16),
            pltpu.VMEM((ni, nk), F32),
            pltpu.VMEM((4 * hq, cc), BF16),
            pltpu.VMEM((ni, nk, cc), BF16),
            pltpu.VMEM((ni, hq, nk), F32),
            pltpu.VMEM((ni, hq, nk), F32),
            pltpu.VMEM((2, nc, ni, nk), BF16),
            pltpu.VMEM((2, nc, ni, nk), BF16),
            pltpu.VMEM((nr, n, nj), BF16),
            pltpu.VMEM((2, npl, 2, ni, nk), BF16),
            pltpu.VMEM((2, npl, 2, ni, nk), BF16),
            pltpu.VMEM((2, npl, ni, nk), F32),
            pltpu.VMEM((2, t_n // 2, nz, hq, nk), BF16),
            pltpu.VMEM((2, t_n // 2, nz, hq, nk), BF16),
            pltpu.VMEM((nr, nq, 4 // nr * hq, cc), BF16),
            pltpu.VMEM((2, nq * 2 * hq, cc), BF16),
            pltpu.VMEM((t_n, nk, cc), F32),
            pltpu.VMEM((t_n, 4, nq, hq, nk), F32),
            pltpu.VMEM((t_n, nk, cc), F32),
            pltpu.VMEM((t_n, nk, cc), F32),
            pltpu.VMEM((2, nq * 2 * hq, t_n * nk), BF16),
            pltpu.VMEM((nq, t_n, nk, cc), BF16),
            pltpu.VMEM((npl, nq, 8, cc), F32),
            pltpu.VMEM((npl, nq, 8, cc), F32),
            pltpu.VMEM((nq, 8, cc), F32),
            pltpu.VMEM((nq // nr, 8, cc), F32),
            pltpu.VMEM((nz, 8, cc), F32),
            pltpu.VMEM((nr, nq // nr, 8, cc), F32),
            pltpu.VMEM((npl, 8, cc), F32),
            dma(6), dma(nq, t_n),
            dma(nc), dma(nc), dma(nr), dma(nr), dma(nq), dma(nq), dma(nr), dma(nr),
            dma(2, nc), dma(2, nc), dma(2, npl), dma(2, npl),
            dma(2, t_n // 2, nz), dma(2, t_n // 2, nz),
            dma(2, nq, t_n), dma(nq, t_n),
            dma(npl), dma(npl), dma(nr), dma(nr), dma(2, nq // nr), dma(nz), dma(nr), dma(1),
            dma(npl), dma(npl),
        ],
        compiler_params=pltpu.CompilerParams(
            collective_id=0, has_side_effects=True, vmem_limit_bytes=60 * 1024 * 1024,
        ),
        name="triangle_backward",
    )(token_mask.reshape(n // nk, nk), pair, pair_mask, ln_gain.reshape(1, cc), wt, grad_tri)
    w_grad = jnp.transpose(wout.reshape(4, hq, cc), (2, 0, 1))
    return out, w_grad


def solution(mesh):
    size = dict(mesh.shape)
    return jax.shard_map(
        functools.partial(body, size["row"], size["col"], size["ch"]),
        mesh=mesh,
        in_specs=(
            P("col", "row", None),
            P(),
            P("col", "row"),
            P(),
            P(None, None, "ch"),
            P("ch", "col", None),
        ),
        out_specs=(P("col", "row", None), P(None, None, "ch")),
        check_vma=False,
    )
```

```python
import functools

import jax
import jax.numpy as jnp
from jax import lax
from jax.experimental import pallas as pl
from jax.experimental.pallas import tpu as pltpu
from jax.sharding import PartitionSpec as P

EPS = 1e-05
F32 = jnp.float32
BF16 = jnp.bfloat16
MESH = pl.DeviceIdType.MESH
NT = (((1,), (1,)), ((), ()))
TN = (((0,), (0,)), ((), ()))


def normalise(x):
    mean = jnp.mean(x, axis=-1, keepdims=True)
    cen = x - mean
    inv = lax.rsqrt(jnp.mean(cen * cen, axis=-1, keepdims=True) + EPS)
    return cen * inv, inv


def factors(p, m):
    p0, p1, p2, p3 = p
    s1 = jax.nn.sigmoid(p1)
    s3 = jax.nn.sigmoid(p3)
    f0 = m * s1
    f2 = m * s3
    return f0, f0 * p0 * (1.0 - s1), f2, f2 * p2 * (1.0 - s3)


def kernel(
    nr, nc, nq,
    tok, pair_h, pm_h, gain_h, w_h, gt,
    out, wout,
    tok_v, pair, pm, gain, w_v, gq, mask, wt,
    normed, lt, rt, lrs, lrr, gfull, dsend, drecv, df, asend, arecv,
    wf, wfs, dno, fo, stdo, invo, gro, ag, wp, wr, zp, zq, zr, xr, wg,
    in_s, o_s,
    g1_s, g1_r, g2_s, g2_r, wf_s, wf_r, wx2_s, wx2_r, lr_s, lr_r, d_s, d_r, a_s, a_r,
    ag_s, ag_r, wa_s, wa_r, wx_s, wx_r, wz_s, wz_r, wb_s, wb_r, wd_s, wd_r,
):
    r = lax.axis_index("row")
    c = lax.axis_index("col")
    q = lax.axis_index("ch")
    ni, nk, cc = pair.shape
    hq = nc
    n = nc * ni
    nj = gfull.shape[2]
    t_n = ni // nq
    jpb = nj // ni
    gr_n = 4 // nr
    wr_n = gr_n * hq
    npl = nc // 2
    nz = 2 * nq
    zh = lax.rem(lax.div(c, 2), 2)
    m = lax.div(c, 4) * 2 + lax.rem(c, 2)
    z = zh * nq + q

    def col_of(zh_, m_):
        return (lax.div(m_, 2) * 2 + zh_) * 2 + lax.rem(m_, 2)

    def pos(c_):
        return lax.rem(lax.div(c_, 2), 2) * npl + lax.div(c_, 4) * 2 + lax.rem(c_, 2)

    def to_row(i):
        return {"row": i}

    def to_col(i):
        return {"col": i}

    def to_ch(i):
        return {"ch": i}

    def to_plane(i):
        return {"col": col_of(zh, i)}

    def to_z(i):
        return {"col": col_of(lax.div(i, nq), m), "ch": lax.rem(i, nq)}

    lane = pl.ds(pl.multiple_of(r * nj, nj), nj)
    mine = pltpu.make_async_copy(gt.at[:, :, lane], gq, in_s.at[5])
    mine.start()
    loads = [
        pltpu.make_async_copy(src, dst, in_s.at[k])
        for k, (src, dst) in enumerate(
            ((w_h, w_v), (tok, tok_v), (pm_h, pm), (gain_h, gain), (pair_h, pair)))
    ]
    for load in loads:
        load.start()

    barrier = pltpu.get_barrier_semaphore()

    def greet(device):
        pl.semaphore_signal(barrier, inc=1, device_id=device, device_id_type=MESH)

    def greet_all(size, me, to):
        def one(off, carry):
            greet(to(lax.rem(me + off, size)))
            return carry
        lax.fori_loop(1, size, one, 0)

    greet_all(nr, r, to_row)
    greet_all(nc, c, to_col)
    greet_all(nq, q, to_ch)

    def greet_far(off, carry):
        greet({"col": col_of(1 - zh, m), "ch": lax.rem(q + off, nq)})
        return carry
    lax.fori_loop(1, nq, greet_far, 0)

    def permuted(w):
        rows = []
        for g in range(4):
            for half in range(2):
                for y in range(nc // 4):
                    at = g * hq + (y * 2 + half) * 2
                    rows.append(w[at:at + 2])
        return jnp.concatenate(rows, axis=0)

    def natural(w):
        rows = []
        for g in range(4):
            for y in range(nc // 4):
                for half in range(2):
                    at = g * hq + half * npl + y * 2
                    rows.append(w[at:at + 2])
        return jnp.concatenate(rows, axis=0)

    def remote(src, dst, s, rr, device):
        return pltpu.make_async_remote_copy(
            src_ref=src, dst_ref=dst, send_sem=s, recv_sem=rr,
            device_id=device, device_id_type=MESH,
        )

    def spread(size, me, make, start=True):
        def one(off, carry):
            to = lax.rem(me + off, size)
            copy = make(to, me)
            if start:
                copy.start()
            else:
                copy.wait_send()
            return carry
        lax.fori_loop(1, size, one, 0)

    def gather(size, me, make):
        def one(off, carry):
            src = lax.rem(me + off, size)
            make(src, src).wait_recv()
            return carry
        lax.fori_loop(1, size, one, 0)


    def rows_of(b):
        return pl.ds(pl.multiple_of(b * ni, ni), ni)

    def g1(to, src):
        return remote(gq.at[to], gfull.at[r, rows_of(src)],
                      g1_s.at[to], g1_r.at[src], to_col(to))

    def g2(to, src):
        return remote(gfull.at[src], gfull.at[src], g2_s.at[to], g2_r.at[src], to_row(to))

    def wfc(to, src):
        part = wt.at[pl.ds(pl.multiple_of(r * wr_n, wr_n), wr_n)]
        return remote(part, wf.at[r, src], wf_s.at[to], wf_r.at[src], to_ch(to))

    def wfx(to, src):
        return remote(wf.at[src], wf.at[src], wx2_s.at[to], wx2_r.at[src], to_row(to))

    def lrc(side):
        def make(to, src):
            return remote(lrs.at[side, pos(to)], lrr.at[side, src],
                          lr_s.at[side, to], lr_r.at[side, src], to_col(to))
        return make

    def dc(side):
        def make(to, src):
            return remote(dsend.at[side, to], drecv.at[side, src],
                          d_s.at[side, to], d_r.at[side, src], to_plane(to))
        return make

    def ac(side, u):
        def make(to, src):
            return remote(asend.at[side, u, to], arecv.at[side, u, src],
                          a_s.at[side, u, to], a_r.at[side, u, src], to_z(to))
        return make

    def wa(to, src):
        return remote(wp.at[to], wr.at[src], wa_s.at[to], wa_r.at[src], to_plane(to))

    qr = nq // nr
    owner = lax.div(q, qr) == r

    def wx(to, src):
        return remote(zp.at[pl.ds(to * qr, qr)], xr.at[src], wx_s.at[to], wx_r.at[src],
                      to_row(to))

    def wz(half, a):
        to = half * nq + r * qr + a
        return to, remote(zq.at[a], zr.at[z], wz_s.at[half, a], wz_r.at[z], to_z(to))

    def wz_from(to, src):
        return remote(zq.at[0], zr.at[src], wz_s.at[0, 0], wz_r.at[src], to_z(to))

    def wb(to, src):
        return remote(wg.at[m], wg.at[m], wb_s.at[to], wb_r.at[0], to_row(to))

    def wd(to, src):
        return remote(wg.at[src], wg.at[src], wd_s.at[to], wd_r.at[src], to_plane(to))

    pl.semaphore_wait(barrier, nr + nc + 2 * nq - 4)
    mine.wait()
    spread(nc, c, g1)
    for load in loads:
        load.wait()
    wv = permuted(w_v[...].astype(F32)).astype(BF16)
    wt[...] = wv
    wf[r, q] = wt[pl.ds(pl.multiple_of(r * wr_n, wr_n), wr_n), :]

    tok_k = tok_v[pl.ds(r, 1), :]
    first = c * ni
    tok_i = tok_v[pl.ds(lax.div(first, nk), 1), :]
    at = lax.broadcasted_iota(jnp.int32, (ni, nk), 1) - lax.rem(first, nk)
    hit = at == lax.broadcasted_iota(jnp.int32, (ni, nk), 0)
    tok_i = jnp.sum(jnp.where(hit, tok_i, 0).astype(F32), axis=1, keepdims=True)
    mask[...] = (pm[...] * tok_k).astype(F32) * tok_i
    gain_v = gain[...]

    spread(nq, q, wfc)
    gfull[r, rows_of(c)] = gq[c]

    def mask_of(i):
        return mask[pl.ds(i, 1), :]

    def project(i, carry):
        std, _ = normalise(pair[i].astype(F32))
        nb = (std * gain_v).astype(BF16)
        normed[i] = nb
        p = lax.dot_general(wt[...], nb, NT, preferred_element_type=F32)
        p = p.reshape(4, hq, nk)
        mk = mask_of(i)
        lt[i] = mk * jax.nn.sigmoid(p[1]) * p[0]
        rt[i] = mk * jax.nn.sigmoid(p[3]) * p[2]
        return carry

    lax.fori_loop(0, ni, project, 0, unroll=4)

    for side, made in ((0, lt), (1, rt)):
        for h in range(hq):
            lrs[side, h] = made[:, h, :].astype(BF16)
        spread(nc, c, lrc(side))
        lrr[side, c] = lrs[side, pos(c)]

    gather(nc, c, g1)
    spread(nr, r, g2)

    gather(nq, q, wfc)
    spread(nr, r, wfx)
    gather(nr, r, wfx)

    def own(t, carry):
        i = q * t_n + t
        std, inv = normalise(pair[i].astype(F32))
        stdo[t] = std
        invo[t] = jnp.broadcast_to(inv, (nk, cc))
        p = lax.dot_general(wf[...].reshape(nq * 4 * hq, cc), normed[i], NT,
                            preferred_element_type=F32)
        p = p.reshape(nr, nq, gr_n, hq, nk)
        f = factors(tuple(p[g // gr_n, :, g % gr_n] for g in range(4)), mask_of(i))
        for g in range(4):
            fo[t, g] = f[g]
        return carry

    tu = t_n // 2

    def return_side(side, d):
        for cb in range(nc):
            dsend[side, cb // 4 * 2 + cb % 2, cb // 2 % 2] = d[cb]
        spread(npl, m, dc(side))
        drecv[side, m] = dsend[side, m]

    def forward_side(side):
        gather(npl, m, dc(side))
        for half in range(2):
            df[half] = drecv[side, :, half].astype(F32)
        for u in range(tu):
            for half in range(2):
                for b in range(nq):
                    i = b * t_n + 2 * u
                    asend[side, u, half * nq + b] = jnp.concatenate(
                        [df[half, :, i, :], df[half, :, i + 1, :]], axis=0).astype(BF16)
            spread(nz, z, ac(side, u))
            arecv[side, u, z] = asend[side, u, z]

    lax.fori_loop(0, tu, own, 0)
    gather(nr, r, g2)
    gather(nc, c, lrc(0))
    left_all = lrr[0].reshape(n, nk)
    dr = []
    for x in range(nr):
        d = lax.dot_general(gfull[x], left_all, TN, preferred_element_type=F32)
        dr.append(d.astype(BF16).reshape(jpb, ni, nk))
    return_side(1, [dr[cb // jpb][cb % jpb] for cb in range(nc)])
    lax.fori_loop(tu, t_n, own, 0)
    for side in range(2):
        for b in range(nq):
            for gg in range(2):
                g, row = side * 2 + gg, (b * 2 + gg) * hq
                at = g % gr_n * hq
                wfs[side, row:row + hq] = wf[g // gr_n, b, at:at + hq]
    forward_side(1)

    gather(nc, c, lrc(1))
    dl = jnp.zeros((n, nk), F32)
    for x in range(nr):
        rx = lrr[1, x * jpb:(x + 1) * jpb].reshape(nj, nk)
        dl = dl + jnp.dot(gfull[x], rx, preferred_element_type=F32)
    dl = dl.astype(BF16).reshape(nc, ni, nk)
    return_side(0, [dl[cb] for cb in range(nc)])
    forward_side(0)

    def side_grads(side, t):
        u, at = t // 2, t % 2 * npl
        d = jnp.stack([
            jnp.stack([arecv[side, u, half * nq + b].astype(F32)[at:at + npl]
                       for half in range(2)])
            for b in range(nq)]).reshape(nq, hq, nk)
        gr = jnp.stack([d * fo[t, 2 * side], d * fo[t, 2 * side + 1]], axis=1)
        gr = gr.reshape(nq * 2 * hq, nk).astype(BF16)
        gro[side, :, t * nk:(t + 1) * nk] = gr
        return lax.dot_general(gr, wfs[side], TN, preferred_element_type=F32)

    def w_side(side):
        nb = normed[pl.ds(q * t_n, t_n)].reshape(t_n * nk, cc)
        part = jnp.dot(gro[side], nb, preferred_element_type=F32)
        part = part.reshape(nq, npl // 2, 8, cc)
        for b in range(npl // 2):
            wp[side * (npl // 2) + b] = part[:, b]

    for u in range(tu):
        gather(nz, z, ac(1, u))
    for t in range(t_n):
        dno[t] = side_grads(1, t)
    w_side(1)

    def to_right(b, t):
        return remote(ag.at[b, t], ag.at[b, t], ag_s.at[0, b, t], ag_r.at[b, t],
                      to_ch(lax.rem(q + 1, nq)))

    def to_left(b, t):
        return remote(ag.at[b, t], ag.at[b, t], ag_s.at[1, b, t], ag_r.at[b, t],
                      to_ch(lax.rem(q + nq - 1, nq)))

    def keep(b, t):
        return pltpu.make_async_copy(ag.at[b, t], out.at[b * t_n + t], o_s.at[b, t])

    def relay_one(s, t):
        @pl.when(q >= s)
        def _():
            to_right(q - s, t).wait_recv()

            @pl.when(q < nq - 1)
            def _():
                to_right(q - s, t).start()
            keep(q - s, t).start()

        @pl.when(q + s < nq)
        def _():
            to_left(q + s, t).wait_recv()

            @pl.when(q > 0)
            def _():
                to_left(q + s, t).start()
            keep(q + s, t).start()

    def relay(s):
        def one(t, carry):
            relay_one(s, t)
            return carry
        lax.fori_loop(0, t_n, one, 0)

    for t in range(t_n):
        if t % 2 == 0:
            gather(nz, z, ac(0, t // 2))
        e = (side_grads(0, t) + dno[t]) * gain_v
        std = stdo[t]
        first = jnp.mean(e, axis=-1, keepdims=True)
        second = jnp.mean(e * std, axis=-1, keepdims=True)
        ag[q, t] = (invo[t] * (e - first - std * second)).astype(BF16)
        keep(q, t).start()

        @pl.when(q < nq - 1)
        def _():
            to_right(q, t).start()

        @pl.when(q > 0)
        def _():
            to_left(q, t).start()

    def w_own():
        w_side(0)
        spread(npl, m, wa)
        wr[m] = wp[m]

    def w_plane():
        gather(npl, m, wa)
        zp[...] = jnp.sum(wr[...], axis=0)
        spread(nr, r, wx)
        xr[r] = zp[pl.ds(r * qr, qr)]

    def w_rows():
        gather(nr, r, wx)
        total = xr[0]
        for x in range(1, nr):
            total = total + xr[x]
        zq[...] = total
        for half in range(2):
            for a in range(qr):
                to, copy = wz(half, a)

                @pl.when(to != z)
                def _(copy=copy):
                    copy.start()

                @pl.when(to == z)
                def _(a=a):
                    zr[z] = zq[a]

    def w_ring():
        @pl.when(owner)
        def _():
            gather(nz, z, wz_from)
            wg[m] = jnp.sum(zr[...], axis=0) * (1.0 / n)
            spread(nr, r, wb)

    def w_share():
        @pl.when(jnp.logical_not(owner))
        def _():
            wb(r, r).wait_recv()
        spread(npl, m, wd)

    def w_last():
        gather(npl, m, wd)

    steps = {0: [w_own], 1: [w_plane], 2: [w_rows], 3: [w_ring], 4: [w_share]}
    done = set()
    for s in range(nq):
        if s > 0:
            relay(s)
        for step in steps.get(s, ()):
            step()
            done.add(step)
    for at in sorted(steps):
        for step in steps[at]:
            if step not in done:
                step()
    w_last()
    wout[...] = natural(wg[...].reshape(4 * hq, cc))

    spread(nc, c, g1, False)
    spread(nq, q, wfc, False)
    spread(nr, r, wfx, False)
    for side in range(2):
        spread(nc, c, lrc(side), False)
    spread(nr, r, g2, False)
    for side in range(2):
        spread(npl, m, dc(side), False)
        for u in range(tu):
            spread(nz, z, ac(side, u), False)
    spread(npl, m, wa, False)
    spread(nr, r, wx, False)
    for half in range(2):
        for a in range(qr):
            to, copy = wz(half, a)

            @pl.when(to != z)
            def _(copy=copy):
                copy.wait_send()

    @pl.when(owner)
    def _():
        spread(nr, r, wb, False)
    spread(npl, m, wd, False)

    def drain(b, carry):
        def one(t, carry):
            @pl.when(jnp.logical_and(b <= q, q < nq - 1))
            def _():
                to_right(b, t).wait_send()

            @pl.when(jnp.logical_and(b >= q, q > 0))
            def _():
                to_left(b, t).wait_send()
            keep(b, t).wait()
            return carry
        return lax.fori_loop(0, t_n, one, carry)
    lax.fori_loop(0, nq, drain, 0)


def body(nr, nc, nq, pair, token_mask, pair_mask, ln_gain, w_in, grad_tri):
    ni, nk, cc = pair.shape
    hq = w_in.shape[2]
    n = nc * ni
    nj = n // nr
    t_n = ni // nq
    npl = nc // 2
    nz = 2 * nq
    wt = jnp.transpose(w_in, (1, 2, 0)).reshape(4 * hq, cc)
    vmem = pl.BlockSpec(memory_space=pltpu.VMEM)
    hbm = pl.BlockSpec(memory_space=pltpu.HBM)
    dma = lambda *s: pltpu.SemaphoreType.DMA(s)
    out, wout = pl.pallas_call(
        functools.partial(kernel, nr, nc, nq),
        out_shape=(
            jax.ShapeDtypeStruct((ni, nk, cc), BF16),
            jax.ShapeDtypeStruct((4 * hq, cc), F32),
        ),
        in_specs=[hbm] * 6,
        out_specs=(hbm, vmem),
        scratch_shapes=[
            pltpu.VMEM((n // nk, nk), jnp.int32),
            pltpu.VMEM((ni, nk, cc), BF16),
            pltpu.VMEM((ni, nk), jnp.int32),
            pltpu.VMEM((1, cc), F32),
            pltpu.VMEM((4 * hq, cc), BF16),
            pltpu.VMEM((nc, ni, nj), BF16),
            pltpu.VMEM((ni, nk), F32),
            pltpu.VMEM((4 * hq, cc), BF16),
            pltpu.VMEM((ni, nk, cc), BF16),
            pltpu.VMEM((ni, hq, nk), F32),
            pltpu.VMEM((ni, hq, nk), F32),
            pltpu.VMEM((2, nc, ni, nk), BF16),
            pltpu.VMEM((2, nc, ni, nk), BF16),
            pltpu.VMEM((nr, n, nj), BF16),
            pltpu.VMEM((2, npl, 2, ni, nk), BF16),
            pltpu.VMEM((2, npl, 2, ni, nk), BF16),
            pltpu.VMEM((2, npl, ni, nk), F32),
            pltpu.VMEM((2, t_n // 2, nz, hq, nk), BF16),
            pltpu.VMEM((2, t_n // 2, nz, hq, nk), BF16),
            pltpu.VMEM((nr, nq, 4 // nr * hq, cc), BF16),
            pltpu.VMEM((2, nq * 2 * hq, cc), BF16),
            pltpu.VMEM((t_n, nk, cc), F32),
            pltpu.VMEM((t_n, 4, nq, hq, nk), F32),
            pltpu.VMEM((t_n, nk, cc), F32),
            pltpu.VMEM((t_n, nk, cc), F32),
            pltpu.VMEM((2, nq * 2 * hq, t_n * nk), BF16),
            pltpu.VMEM((nq, t_n, nk, cc), BF16),
            pltpu.VMEM((npl, nq, 8, cc), F32),
            pltpu.VMEM((npl, nq, 8, cc), F32),
            pltpu.VMEM((nq, 8, cc), F32),
            pltpu.VMEM((nq // nr, 8, cc), F32),
            pltpu.VMEM((nz, 8, cc), F32),
            pltpu.VMEM((nr, nq // nr, 8, cc), F32),
            pltpu.VMEM((npl, 8, cc), F32),
            dma(6), dma(nq, t_n),
            dma(nc), dma(nc), dma(nr), dma(nr), dma(nq), dma(nq), dma(nr), dma(nr),
            dma(2, nc), dma(2, nc), dma(2, npl), dma(2, npl),
            dma(2, t_n // 2, nz), dma(2, t_n // 2, nz),
            dma(2, nq, t_n), dma(nq, t_n),
            dma(npl), dma(npl), dma(nr), dma(nr), dma(2, nq // nr), dma(nz), dma(nr), dma(1),
            dma(npl), dma(npl),
        ],
        compiler_params=pltpu.CompilerParams(
            collective_id=0, has_side_effects=True, vmem_limit_bytes=60 * 1024 * 1024,
        ),
        name="triangle_backward",
    )(token_mask.reshape(n // nk, nk), pair, pair_mask, ln_gain.reshape(1, cc), wt, grad_tri)
    w_grad = jnp.transpose(wout.reshape(4, hq, cc), (2, 0, 1))
    return out, w_grad


def solution(mesh):
    size = dict(mesh.shape)
    return jax.shard_map(
        functools.partial(body, size["row"], size["col"], size["ch"]),
        mesh=mesh,
        in_specs=(
            P("col", "row", None),
            P(),
            P("col", "row"),
            P(),
            P(None, None, "ch"),
            P("ch", "col", None),
        ),
        out_specs=(P("col", "row", None), P(None, None, "ch")),
        check_vma=False,
    )
```
